128 devices in a mesh: src: 4 (over x), rcv: 32 (over z, y, core).
Axes of the slice: x: 4, y: 4, z: 4, core: 2. Of those that a mesh axis runs over, the one named last changes fastest.
Arguments:
- traces: bfloat16 [4096, 512], P('rcv'), may hold values from -6 to 6
- band_group: int32 [4096], P('rcv'), may hold values from 0 to 23
- filters: float32 [24, 32], replicated, may hold values from -1 to 1
- pair_bin: int32 [2, 512, 4096], P(None, 'src', 'rcv'), may hold values from 0 to 1023, as said below
- bin_order: int32 [1024], replicated, may hold values from 0 to 1023, each once
Outputs:
- bin_stacks: float32 [1024, 512], P(('src', 'rcv'))
The draws below stay inside these ranges and needn't reach their ends.
Inputs may be any that keep to these rules, and one draw needn't show every extreme that they name: pair_bin[k, p, c] is the distance along the fiber between the source channel of row p at step k and channel c, in bins of 4 channel spacings, where the spacing between neighbouring channels varies by up to a half; every bin number appears; for one step, one block of 128 source rows and one block of 128 receiver channels, the bins lie within 66 consecutive values.
All inputs are finite; a program needn't handle non-finite values.
Results may differ from the reference program's by a relative error of at most 0.0037.
Values may be sent and summed in bfloat16 or wider, within the bound.
No kernel may reach another device: no remote copies, remote signals or barrier semaphores. Data moves between devices by JAX's collectives and lax.ppermute only.
A program may use at most 256 MiB of HBM per device.

```python
import jax
import jax.numpy as jnp
from jax import lax

CH_DEV = 128
SAMPLES = 512
LAGS = 512
LAGBLK = 128
BANDS = 24
TAPS = 32
STEPS = 2
CH = 4096
SRC_ROWS = 512
NBINS = 1024
N_SRC = 4
N_RCV = 32


def draw_pair_bin(key, part):
    key = jax.random.fold_in(key, 11)
    jitter = jax.random.randint(key, (CH,), -2, 3, dtype=jnp.int32)
    places = jnp.arange(CH, dtype=jnp.int32) * 8 + jitter
    stride = N_RCV // (STEPS * N_SRC)
    width = 8 * (CH // NBINS)
    step_index = jnp.arange(STEPS, dtype=jnp.int32)[:, None]
    row_index = jnp.arange(SRC_ROWS, dtype=jnp.int32)[None, :]
    source_channel = (step_index * N_SRC + row_index // CH_DEV) * stride * CH_DEV + row_index % CH_DEV
    source_place = places[source_channel]
    distance = jnp.abs(source_place[:, :, None] - places[None, None, :])
    return jnp.minimum(distance // width, NBINS - 1).astype(jnp.int32)


def touch_ends(array, stream_key, low, largest):
    index_at = [jax.random.randint(jax.random.fold_in(stream_key, axis), (), 0, length) for axis, length in enumerate(array.shape)]
    main_axis = array.shape.index(max(array.shape))
    neighbour = index_at[:main_axis] + [(index_at[main_axis] + 1) % array.shape[main_axis]] + index_at[main_axis + 1:]
    return array.at[tuple(index_at)].set(low).at[tuple(neighbour)].set(largest)


def level_of(stream_key, extent, split, least, high):
    loudness, own = 1.0, jax.random.fold_in(stream_key, 6)
    for axis_at, parts in split:
        draws = jnp.exp(jax.random.uniform(jax.random.fold_in(own, axis_at), (parts,), jnp.float32, least / len(split), high / len(split)))
        loudness = loudness * jnp.repeat(draws, extent[axis_at] // parts).reshape([-1 if axis == axis_at else 1 for axis in range(len(extent))])
    return loudness


def centred(own_key, dims, deviation, bound, split=(), held_as=jnp.bfloat16):
    level = level_of(own_key, dims, split, -0.22, 0.18) if split else 1.0
    values = jax.random.normal(own_key, dims, jnp.float32) * deviation * level
    return jnp.minimum(jnp.maximum(values, -bound), bound).astype(held_as)


def setup_inputs(seed: int = 0) -> dict:
    arg_keys = jax.random.split(jax.random.key(seed), 6)
    traces = centred(arg_keys[0], (CH, SAMPLES), 1.0, 6.0, ((0, 32),))
    band_group = touch_ends(jax.random.randint(arg_keys[1], (CH,), 0, BANDS), jax.random.fold_in(arg_keys[1], 1), 0, BANDS - 1).astype(jnp.int32)
    filters = centred(arg_keys[2], (BANDS, TAPS), TAPS ** -0.5, 1.0, (), jnp.float32)
    pair_bin = draw_pair_bin(jax.random.fold_in(arg_keys[5], 71), 0)
    bin_order = jax.random.permutation(arg_keys[4], NBINS).astype(jnp.int32)
    return dict(traces=traces, band_group=band_group, filters=filters, pair_bin=pair_bin, bin_order=bin_order)


def prefilter(traces, band_group, filters):
    onehot = (band_group[:, None] == jnp.arange(BANDS, dtype=jnp.int32)[None, :]).astype(jnp.float32)
    taps = jnp.dot(onehot, filters.astype(jnp.float32), precision=lax.Precision.HIGHEST)
    signal = traces.astype(jnp.float32)
    padded = jnp.pad(signal, ((0, 0), (TAPS - 1, 0)))
    length = signal.shape[1]
    output = jnp.zeros_like(signal)
    for step in range(TAPS):
        output = output + taps[:, step:step + 1] * padded[:, TAPS - 1 - step:TAPS - 1 - step + length]
    scale = lax.rsqrt(lax.optimization_barrier(jnp.mean(output * output, axis=1, keepdims=True)) + 1e-06)
    return (output * scale).astype(jnp.bfloat16)

def hankel_rows(window):
    rows, width = window.shape
    half = width // 2
    tiled = jnp.tile(window, (1, half))
    tiled = jnp.pad(tiled, ((0, 0), (0, half)))
    return tiled.reshape(rows, half, width + 1)[:, :, :half]

def build_hankel(receivers):
    rows, length = receivers.shape
    padded = jnp.pad(receivers, ((0, 0), (LAGS // 2, LAGS // 2)))
    blocks = padded.reshape(rows, (length + LAGS) // LAGBLK, LAGBLK)
    windows = jnp.concatenate([blocks[:, :-1], blocks[:, 1:]], axis=2)
    return lax.map(hankel_rows, jnp.transpose(windows, (1, 0, 2)))

def correlate_bins(source, hankel, bins, nbins):
    rows, length = source.shape
    nblocks = length // LAGBLK
    shaped = source.astype(jnp.float32).reshape(rows, nblocks, LAGBLK)
    flat_bins = bins.reshape(-1)
    pieces = []
    for shift in range(LAGS // LAGBLK):
        corr = jnp.einsum('ibu,bjum->ijm', shaped, hankel[shift:shift + nblocks])
        pieces.append(jax.ops.segment_sum(corr.reshape(-1, LAGBLK), flat_bins, num_segments=nbins))
    return jnp.concatenate(pieces, axis=1)

def reference(traces, band_group, filters, pair_bin, bin_order):
    filtered = prefilter(traces, band_group, filters)
    stride = N_RCV // (STEPS * N_SRC)
    blocks = filtered.reshape(N_RCV, CH_DEV, SAMPLES)
    sources = jnp.stack([blocks[(step * N_SRC + group) * stride] for step in range(STEPS) for group in range(N_SRC)])
    shaped_bins = pair_bin.reshape(STEPS, N_SRC, CH_DEV, N_RCV, CH_DEV)
    shaped_bins = jnp.transpose(shaped_bins, (3, 0, 1, 2, 4)).reshape(N_RCV, STEPS * N_SRC, CH_DEV, CH_DEV)

    def accumulate(total, item):
        receivers, bins = item
        hankel = build_hankel(receivers).astype(jnp.float32)
        for number in range(STEPS * N_SRC):
            total = total + correlate_bins(sources[number], hankel, bins[number], NBINS)
        return (total, None)
    sums, unused = lax.scan(accumulate, jnp.zeros((NBINS, LAGS), jnp.float32), (blocks, shaped_bins))
    flat_bins = pair_bin.reshape(-1)
    counts = jax.ops.segment_sum(jnp.ones(flat_bins.shape, jnp.float32), flat_bins, num_segments=NBINS)
    ordered = sums[bin_order]
    return ordered / jnp.sqrt(SAMPLES * counts[bin_order])[:, None]
```

```python
import functools

import jax
import jax.numpy as jnp
import numpy as np
from jax import lax
from jax.experimental import pallas as pl
from jax.experimental.pallas import tpu as pltpu
from jax.sharding import PartitionSpec as P

LAGS = 512
SAMPLES = 512
TAPS = 32
FREQS = 384
PERIOD = 2 * FREQS
CH = 128
GROUP = 8
SPAN = 72
WIN = 128
RING = 4
BF = jnp.bfloat16
F32 = jnp.float32


def split_bf16(matrix):
    high = matrix.astype(np.float32).astype(jnp.bfloat16)
    low = (matrix - high.astype(np.float64)).astype(np.float32).astype(jnp.bfloat16)
    return np.stack([high, low])


@functools.lru_cache(None)
def transforms():
    odd = 2 * np.arange(FREQS) + 1
    t = np.arange(SAMPLES)
    angle = np.pi / PERIOD * ((t[:, None] * odd[None, :]) % (2 * PERIOD))
    forward = np.concatenate([np.cos(angle), -np.sin(angle)], axis=1)
    lag = np.arange(LAGS) - LAGS // 2
    angle = np.pi / PERIOD * ((odd[:, None] * lag[None, :]) % (2 * PERIOD))
    back = np.concatenate([np.cos(angle), -np.sin(angle)], axis=0) * (2.0 / PERIOD)
    return split_bf16(forward), split_bf16(back)


def device(src, z, y, core):
    return src * 32 + (z % RING) * 8 + (y % RING) * 2 + core


def owners():
    for s in range(4):
        for k in range(2):
            yield s, k, 2 * (s % 2), 2 * k + s // 2


def plans():
    first, second = [], []
    for s, k, y, z in owners():
        first.append((device(s, z, y, k), device(s, z, y + 1, k)))
        first.append((device(s, z, y, 1 - k), device(s, z, y - 1, k)))
        second.append((device(s, z, y, k), device(s, z, y + 2, k)))
    along = []
    for d in (1, 3, 2):
        along.append(
            [
                (device(s, z, yy, k), device(s, z + d, yy, k))
                for s, k, y, z in owners()
                for yy in range(RING)
            ]
        )
    return [first, second], along


def vmem(n):
    return [pl.BlockSpec(memory_space=pltpu.VMEM)] * n


def prefilter_kernel(traces_ref, band_ref, filters_ref, out_ref, pad_ref):
    bands = filters_ref.shape[0]
    onehot = (lax.broadcasted_iota(jnp.int32, (bands, CH), 0) == band_ref[...]).astype(F32)
    taps = lax.dot_general(
        filters_ref[...],
        onehot,
        (((0,), (0,)), ((), ())),
        precision=lax.Precision.HIGHEST,
        preferred_element_type=F32,
    )
    pad_ref[0:TAPS, :] = jnp.zeros((TAPS, CH), F32)
    pad_ref[TAPS:, :] = traces_ref[...].astype(F32).T
    rows = 128
    power = jnp.zeros((1, CH), F32)
    parts = []
    for start in range(0, SAMPLES, rows):
        total = jnp.zeros((rows, CH), F32)
        for k in range(TAPS):
            low = TAPS + start - k
            total = total + taps[k : k + 1, :] * pad_ref[low : low + rows, :]
        power = power + jnp.sum(total * total, axis=0, keepdims=True)
        parts.append(total)
    scale = lax.rsqrt(power * (1.0 / SAMPLES) + 1e-06)
    for i, total in enumerate(parts):
        out_ref[:, i * rows : (i + 1) * rows] = (total * scale).T.astype(BF)


def prefilter(traces, band_group, filters):
    return pl.pallas_call(
        prefilter_kernel,
        out_shape=jax.ShapeDtypeStruct((CH, SAMPLES), BF),
        in_specs=vmem(3),
        out_specs=pl.BlockSpec(memory_space=pltpu.VMEM),
        scratch_shapes=[pltpu.VMEM((TAPS + SAMPLES, CH), F32)],
        name="prefilter",
    )(traces, band_group.reshape(1, CH), filters)


def receivers_kernel(mine_ref, other_ref, w_ref, out_ref):
    for i, ref in enumerate((mine_ref, other_ref)):
        value = jnp.dot(ref[...], w_ref[0], preferred_element_type=F32)
        value = value + jnp.dot(ref[...], w_ref[1], preferred_element_type=F32)
        out_ref[i * CH : (i + 1) * CH, :] = value.astype(BF)


def receivers(mine, other, w):
    return pl.pallas_call(
        receivers_kernel,
        out_shape=jax.ShapeDtypeStruct((2 * CH, PERIOD), BF),
        in_specs=vmem(3),
        out_specs=pl.BlockSpec(memory_space=pltpu.VMEM),
        compiler_params=pltpu.CompilerParams(vmem_limit_bytes=40 * 1024 * 1024),
        cost_estimate=pl.CostEstimate(
            flops=2 * 2 * 2 * CH * SAMPLES * PERIOD, bytes_accessed=2 * 1024 * 1024, transcendentals=0
        ),
        name="receivers",
    )(mine, other, w)


def correlate_kernel(
    low_ref, held_ref, r0, r1, r2, w_ref, fc_ref, bins_ref, back_ref, out_ref, fs, total, g0, g1
):
    block = ((held_ref[...] + r0[...]) + (r1[...] + r2[...])).astype(BF)
    fs[...] = jnp.dot(block, w_ref[0], preferred_element_type=F32) + jnp.dot(
        block, w_ref[1], preferred_element_type=F32
    )
    total[...] = jnp.zeros_like(total)
    n_groups = CH // GROUP

    def spread(g, span, buffer):
        first = pl.multiple_of(g * GROUP, GROUP)
        rel = bins_ref[pl.ds(first, GROUP), :] - low_ref[g]
        offsets = lax.broadcasted_iota(jnp.int32, (span, 2 * CH), 0)
        for p in range(0, GROUP, 2):
            pair = jnp.concatenate(
                [jnp.where(rel[q : q + 1, :] == offsets, 1.0, 0.0) for q in (p, p + 1)], axis=0
            ).astype(BF)
            buffer[p * span : (p + 2) * span, :] = jnp.dot(
                pair, fc_ref[...], preferred_element_type=F32
            )

    def gather(g, span, buffer):
        first = pl.multiple_of(g * GROUP, GROUP)
        low = low_ref[g] - low_ref[n_groups]
        shift = low % 8
        start = pl.multiple_of(low - shift, 8)
        room = jnp.zeros((8, 128), F32)
        for j in range(0, FREQS, 128):
            re, im = slice(j, j + 128), slice(FREQS + j, FREQS + j + 128)
            fr, fi = fs[pl.ds(first, GROUP), re], fs[pl.ds(first, GROUP), im]
            sum_re = jnp.zeros((span, 128), F32)
            sum_im = jnp.zeros((span, 128), F32)
            for p in range(GROUP):
                rows = slice(p * span, (p + 1) * span)
                gr, gi = buffer[rows, re], buffer[rows, im]
                a, b = fr[p : p + 1, :], fi[p : p + 1, :]
                sum_re = sum_re + (a * gr + b * gi)
                sum_im = sum_im + (a * gi - b * gr)
            for part, value in ((re, sum_re), (im, sum_im)):
                moved = pltpu.roll(jnp.concatenate([value, room], axis=0), shift, 0)
                total[pl.ds(start, span + 8), part] += moved

    fits = low_ref[n_groups + 1] == 1

    @pl.when(fits)
    def _():
        spread(0, SPAN, g0)

        def body(h, carry):
            g = 2 * h
            spread(g + 1, SPAN, g1)
            gather(g, SPAN, g0)
            spread(jnp.minimum(g + 2, n_groups - 1), SPAN, g0)
            gather(g + 1, SPAN, g1)
            return carry

        lax.fori_loop(0, n_groups // 2, body, 0)

    @pl.when(jnp.logical_not(fits))
    def _():
        def body(g, carry):
            spread(g, WIN, g0)
            gather(g, WIN, g0)
            return carry

        lax.fori_loop(0, n_groups, body, 0)

    for start in range(0, WIN, 128):
        value = total[start : start + 128, :]
        high = value.astype(BF)
        low = (value - high.astype(F32)).astype(BF)
        out_ref[start : start + 128, :] = (
            jnp.dot(high, back_ref[0], preferred_element_type=F32)
            + jnp.dot(low, back_ref[0], preferred_element_type=F32)
            + jnp.dot(high, back_ref[1], preferred_element_type=F32)
        )


def correlate(lows, held, parts, w, fc, bins, back):
    return pl.pallas_call(
        correlate_kernel,
        out_shape=jax.ShapeDtypeStruct((WIN, LAGS), F32),
        in_specs=[pl.BlockSpec(memory_space=pltpu.SMEM)] + vmem(8),
        out_specs=pl.BlockSpec(memory_space=pltpu.VMEM),
        scratch_shapes=[
            pltpu.VMEM((CH, PERIOD), F32),
            pltpu.VMEM((2 * WIN, PERIOD), F32),
            pltpu.VMEM((GROUP * WIN, PERIOD), F32),
            pltpu.VMEM((GROUP * SPAN, PERIOD), F32),
        ],
        compiler_params=pltpu.CompilerParams(vmem_limit_bytes=40 * 1024 * 1024),
        cost_estimate=pl.CostEstimate(
            flops=2 * 128 * SPAN * 256 * PERIOD, bytes_accessed=6 * 1024 * 1024, transcendentals=0
        ),
        name="correlate",
    )(lows, held, *parts, w, fc, bins, back)


def arrange_kernel(base_ref, order_ref, mine_ref, other_ref, counts_ref, out_ref):
    columns = lax.broadcasted_iota(jnp.int32, (512, WIN), 1)
    order = order_ref[...]
    result = None
    tally = None
    for i, ref in enumerate((mine_ref, other_ref)):
        pick = jnp.where(order - base_ref[i] == columns, 1.0, 0.0).astype(BF)
        value = ref[...]
        high = value.astype(BF)
        low = (value - high.astype(F32)).astype(BF)
        part = jnp.dot(pick, high, preferred_element_type=F32) + jnp.dot(
            pick, low, preferred_element_type=F32
        )
        count = jnp.dot(pick, counts_ref[i], preferred_element_type=F32)
        result = part if result is None else result + part
        tally = count if tally is None else tally + count
    out_ref[:, :LAGS] = result.astype(BF)
    out_ref[:, LAGS:] = tally.astype(BF)


def arrange(bases, order, mine, other, counts):
    return pl.pallas_call(
        arrange_kernel,
        out_shape=jax.ShapeDtypeStruct((512, LAGS + 128), BF),
        in_specs=[pl.BlockSpec(memory_space=pltpu.SMEM)] + vmem(4),
        out_specs=pl.BlockSpec(memory_space=pltpu.VMEM),
        compiler_params=pltpu.CompilerParams(vmem_limit_bytes=40 * 1024 * 1024),
        name="arrange",
    )(bases, order, mine, other, counts)


def finish_kernel(parts_ref, out_ref):
    value = jnp.sum(parts_ref[...].astype(F32).reshape(64, 8, LAGS + 128), axis=0)
    totals = jnp.sum(value[:, LAGS:], axis=1, keepdims=True)
    out_ref[...] = value[:, :LAGS] / jnp.sqrt(SAMPLES * totals)


def finish(parts):
    return pl.pallas_call(
        finish_kernel,
        out_shape=jax.ShapeDtypeStruct((8, LAGS), F32),
        in_specs=vmem(1),
        out_specs=pl.BlockSpec(memory_space=pltpu.VMEM),
        compiler_params=pltpu.CompilerParams(vmem_limit_bytes=40 * 1024 * 1024),
        name="finish",
    )(parts)


def shards(traces, band_group, filters, pair_bin, bin_order):
    both = ("src", "rcv")
    swap = [(i, i ^ 1) for i in range(32)]
    forward, back = transforms()
    w, back = jnp.asarray(forward), jnp.asarray(back)
    src, rcv = lax.axis_index("src"), lax.axis_index("rcv")
    core = rcv % 2
    y, z = (rcv // 2) % RING, rcv // 8
    owner = jnp.logical_and(y == 2 * (src % 2), z == 2 * core + src // 2)

    own_bins = lax.dynamic_index_in_dim(pair_bin, core, 0, keepdims=False)
    other_bins = lax.dynamic_index_in_dim(pair_bin, 1 - core, 0, keepdims=False)
    bins = jnp.concatenate([own_bins, lax.ppermute(other_bins, "rcv", swap)], axis=1)

    filtered = prefilter(traces, band_group, filters)
    partner = lax.ppermute(filtered, "rcv", swap)
    seed = jnp.where(core == 0, filtered, partner)
    across, along = plans()
    got = [lax.ppermute(seed, both, plan) for plan in across]
    held = jnp.where(owner, seed, got[0] + got[1])
    parts = [lax.ppermute(held, both, plan) for plan in along]

    fc = receivers(filtered, partner, w)
    lowest = jnp.min(bins)
    grouped = bins.reshape(CH // GROUP, GROUP * 2 * CH)
    lows, highs = jnp.min(grouped, axis=1), jnp.max(grouped, axis=1)
    fits = jnp.all(highs - lows < SPAN)
    lows = jnp.minimum(jnp.where(fits, lows, lowest), lowest + WIN)
    table = jnp.concatenate([lows, lowest[None], fits.astype(jnp.int32)[None]])
    counts = jnp.sum(
        (bins.reshape(1, -1) - lowest == jnp.arange(WIN, dtype=jnp.int32)[:, None]).astype(jnp.int32),
        axis=1,
    )
    message = jnp.concatenate([counts, lowest[None]])
    theirs = lax.ppermute(message, "rcv", swap)
    tallies = jnp.stack([counts, theirs[:WIN]])
    bases = jnp.stack([lowest, theirs[WIN]])
    lane = jnp.arange(128, dtype=jnp.int32)
    place = jnp.arange(2, dtype=jnp.int32)[:, None, None] * 2
    tallies = tallies[:, :, None]
    tallies = jnp.where(lane == place, tallies // 256 * 256, 0) + jnp.where(
        lane == place + 1, tallies % 256, 0
    )
    tallies = tallies.astype(BF)
    order = lax.dynamic_index_in_dim(bin_order.reshape(64, 2, 8), core, 1, keepdims=False)
    order = order.reshape(512, 1)

    window = correlate(table, held, parts, w, fc, bins, back)
    other_window = lax.ppermute(window, "rcv", swap)
    payload = arrange(bases, order, window, other_window, tallies)
    groups = [[2 * i + c for i in range(64)] for c in range(2)]
    arrived = lax.all_to_all(payload, both, 0, 0, tiled=True, axis_index_groups=groups)
    return finish(arrived)


def solution(mesh):
    in_specs = (P("rcv", None), P("rcv"), P(), P(None, "src", "rcv"), P())
    out_specs = P(("src", "rcv"), None)
    return jax.shard_map(shards, mesh=mesh, in_specs=in_specs, out_specs=out_specs, check_vma=False)
```

```python
import functools

import jax
import jax.numpy as jnp
import numpy as np
from jax import lax
from jax.experimental import pallas as pl
from jax.experimental.pallas import tpu as pltpu
from jax.sharding import PartitionSpec as P

LAGS = 512
SAMPLES = 512
TAPS = 32
FREQS = 384
PERIOD = 2 * FREQS
CH = 128
GROUP = 16
SPAN = 72
WIN = 128
LIMIT = 16 * 1024 * 1024
RING = 4
BF = jnp.bfloat16
F32 = jnp.float32


def split_bf16(matrix):
    high = matrix.astype(np.float32).astype(jnp.bfloat16)
    low = (matrix - high.astype(np.float64)).astype(np.float32).astype(jnp.bfloat16)
    return np.stack([high, low])


@functools.lru_cache(None)
def transforms():
    odd = 2 * np.arange(FREQS) + 1
    t = np.arange(SAMPLES)
    angle = np.pi / PERIOD * ((t[:, None] * odd[None, :]) % (2 * PERIOD))
    forward = np.stack([np.cos(angle), -np.sin(angle)], axis=1).reshape(SAMPLES, 2, -1, 128)
    forward = forward.transpose(0, 2, 1, 3).reshape(SAMPLES, PERIOD)
    lag = np.arange(LAGS) - LAGS // 2
    angle = np.pi / PERIOD * ((odd[:, None] * lag[None, :]) % (2 * PERIOD))
    back = np.stack([np.cos(angle), -np.sin(angle)], axis=0).reshape(2, -1, 128, LAGS)
    back = back.transpose(1, 0, 2, 3).reshape(PERIOD, LAGS) * (2.0 / PERIOD)
    return split_bf16(forward), split_bf16(back)


def device(src, z, y, core):
    return src * 32 + (z % RING) * 8 + (y % RING) * 2 + core


def owners():
    for s in range(4):
        for k in range(2):
            yield s, k, 2 * (s % 2), 2 * k + s // 2


def plans():
    across, up, along = [[], []], [[], []], []
    for s, k, y, z in owners():
        across[0].append((device(s, z, y, 0), device(s, z, y + 2, k)))
        across[1].append((device(s, z, y, 0), device(s, z, y - 1, k)))
        across[1].append((device(s, z, y, 1), device(s, z, y + 1, k)))
        up[0].append((device(s, z, y, 0), device(s, z + 2, y, k)))
        up[1].append((device(s, z, y, 0), device(s, z - 1, y, k)))
        up[1].append((device(s, z, y, 1), device(s, z + 1, y, k)))
    for d in (2, 1, 3):
        along.append(
            [
                (device(s, z, y + yy, k), device(s, z + d, y + yy, k))
                for s, k, y, z in owners()
                for yy in range(1, RING)
            ]
        )
    return across, up, along


def in_hbm(value):
    return pltpu.with_memory_space_constraint(value, pltpu.HBM)


def vmem(n):
    return [pl.BlockSpec(memory_space=pltpu.VMEM)] * n


def prefilter_kernel(traces_ref, band_ref, filters_ref, out_ref, pad_ref):
    bands = filters_ref.shape[0]
    onehot = (lax.broadcasted_iota(jnp.int32, (bands, CH), 0) == band_ref[...]).astype(F32)
    taps = lax.dot_general(
        filters_ref[...],
        onehot,
        (((0,), (0,)), ((), ())),
        precision=lax.Precision.HIGHEST,
        preferred_element_type=F32,
    )
    pad_ref[0:TAPS, :] = jnp.zeros((TAPS, CH), F32)
    pad_ref[TAPS:, :] = traces_ref[...].astype(F32).T
    rows = 128
    power = jnp.zeros((1, CH), F32)
    parts = []
    for start in range(0, SAMPLES, rows):
        total = jnp.zeros((rows, CH), F32)
        for k in range(TAPS):
            low = TAPS + start - k
            total = total + taps[k : k + 1, :] * pad_ref[low : low + rows, :]
        power = power + jnp.sum(total * total, axis=0, keepdims=True)
        parts.append(total)
    scale = lax.rsqrt(power * (1.0 / SAMPLES) + 1e-06)
    for i, total in enumerate(parts):
        out_ref[:, i * rows : (i + 1) * rows] = (total * scale).T.astype(BF)


def prefilter(traces, band_group, filters):
    return pl.pallas_call(
        prefilter_kernel,
        out_shape=pltpu.VMEM((CH, SAMPLES), BF),
        in_specs=vmem(3),
        out_specs=pl.BlockSpec(memory_space=pltpu.VMEM),
        scratch_shapes=[pltpu.VMEM((TAPS + SAMPLES, CH), F32)],
        name="prefilter",
    )(traces, band_group.reshape(1, CH), filters)


def correlate_kernel(
    scalars, low_ref, held_ref, r0, r1, r2, r3, r4, w_ref, fc_ref, bins_ref, hot_ref, back_ref, out_ref,
    fs, total, wide,
):
    held = held_ref[...].astype(F32) * scalars[2].astype(F32)
    rest = (r0[...] + r1[...]) + (r2[...] + r3[...]) + r4[...]
    block = (held + rest.astype(F32)).astype(BF)
    fs[...] = jnp.dot(block, w_ref[0], preferred_element_type=F32) + jnp.dot(
        block, w_ref[1], preferred_element_type=F32
    )
    total[...] = jnp.zeros_like(total)
    n_groups = CH // GROUP

    def spread(hot, j):
        return jnp.dot(hot, fc_ref[:, j * 256 : (j + 1) * 256], preferred_element_type=F32)

    def gather(g, j, span, buffer):
        first = pl.multiple_of(g * GROUP, GROUP)
        low = low_ref[g, 0]
        shift = low % 8
        start = pl.multiple_of(low - shift, 8)
        room = jnp.zeros((8, 128), F32)
        re, im = slice(j * 256, j * 256 + 128), slice(j * 256 + 128, (j + 1) * 256)
        fr, fi = fs[pl.ds(first, GROUP), re], fs[pl.ds(first, GROUP), im]
        sum_re = jnp.zeros((span, 128), F32)
        sum_im = jnp.zeros((span, 128), F32)
        for p in range(GROUP):
            rows = slice(p * span, (p + 1) * span)
            gr, gi = buffer[rows, 0:128], buffer[rows, 128:256]
            a, b = fr[p : p + 1, :], fi[p : p + 1, :]
            sum_re = sum_re + (a * gr + b * gi)
            sum_im = sum_im + (a * gi - b * gr)
        for part, value in ((re, sum_re), (im, sum_im)):
            moved = pltpu.roll(jnp.concatenate([value, room], axis=0), shift, 0)
            total[pl.ds(start, span + 8), part] += moved

    fits = low_ref[n_groups, 0] == 1

    @pl.when(fits)
    def _():
        def body(g, carry):
            for j in range(3):
                gather(g, j, SPAN, spread(hot_ref[g], j))
            return carry

        lax.fori_loop(0, n_groups, body, 0)

    @pl.when(jnp.logical_not(fits))
    def _():
        offsets = lax.broadcasted_iota(jnp.int32, (WIN, 2 * CH), 0)

        def body(g, carry):
            rel = bins_ref[pl.ds(pl.multiple_of(g * GROUP, GROUP), GROUP), :]
            for p in range(GROUP):
                row = jnp.where(rel[p : p + 1, :] == offsets, 1.0, 0.0)
                wide[p * WIN : (p + 1) * WIN, :] = row.astype(BF)
            for j in range(3):
                gather(g, j, WIN, spread(wide[...], j))
            return carry

        lax.fori_loop(0, n_groups, body, 0)

    for start in range(0, WIN, 128):
        value = total[start : start + 128, :]
        high = value.astype(BF)
        low = (value - high.astype(F32)).astype(BF)
        value = (
            jnp.dot(high, back_ref[0], preferred_element_type=F32)
            + jnp.dot(low, back_ref[0], preferred_element_type=F32)
            + jnp.dot(high, back_ref[1], preferred_element_type=F32)
        )
        out_ref[start : start + 128, :] = value.astype(BF)


def correlate(scalars, lows, held, parts, w, fc, bins, hot, back):
    return pl.pallas_call(
        correlate_kernel,
        out_shape=jax.ShapeDtypeStruct((WIN, LAGS), BF),
        in_specs=[pl.BlockSpec(memory_space=pltpu.SMEM)] * 2 + vmem(11),
        out_specs=pl.BlockSpec(memory_space=pltpu.VMEM),
        scratch_shapes=[
            pltpu.VMEM((CH, PERIOD), F32),
            pltpu.VMEM((2 * WIN, PERIOD), F32),
            pltpu.VMEM((GROUP * WIN, 2 * CH), BF),
        ],
        compiler_params=pltpu.CompilerParams(vmem_limit_bytes=LIMIT),
        cost_estimate=pl.CostEstimate(
            flops=2 * 128 * SPAN * 256 * PERIOD, bytes_accessed=6 * 1024 * 1024, transcendentals=0
        ),
        name="correlate",
    )(scalars, lows, held, *parts, w, fc, bins, hot, back)


def survey_kernel(
    scalars, pair_ref, other_ref, mine_ref, partner_ref, w_ref, bins_ref, table_ref, fc_ref, flag_ref,
    raw, w, sems,
):
    core = scalars[0]
    copies = [pltpu.make_async_copy(pair_ref.at[core], raw, sems.at[0])] + [
        pltpu.make_async_copy(w_ref.at[i, pl.ds(j, 128)], w.at[i, pl.ds(j, 128)], sems.at[1 + 4 * i + j // 128])
        for i in range(2)
        for j in range(0, SAMPLES, 128)
    ]
    for copy in copies:
        copy.start()
    flag_ref[...] = jnp.full(flag_ref.shape, scalars[1], jnp.int32)
    copies[0].wait()
    bins = jnp.concatenate([raw[...], other_ref[core]], axis=1)
    lowest = jnp.min(jnp.min(bins, axis=0, keepdims=True), axis=1, keepdims=True)
    rel = bins - lowest
    bins_ref[...] = rel
    n_groups = CH // GROUP
    grouped = rel.reshape(n_groups, GROUP, 2 * CH)
    low = jnp.min(jnp.min(grouped, axis=1), axis=1, keepdims=True)
    high = jnp.max(jnp.max(grouped, axis=1), axis=1, keepdims=True)
    widest = jnp.max(high - low, axis=0, keepdims=True)
    fits = (widest < SPAN).astype(jnp.int32)
    low = jnp.minimum(low * fits, WIN)
    table_ref[0:n_groups, :] = jnp.broadcast_to(low, (n_groups, 128))
    table_ref[n_groups:, :] = jnp.broadcast_to(fits, (8, 128))
    for copy in copies[1:]:
        copy.wait()
    for i, ref in enumerate((mine_ref, partner_ref)):
        value = jnp.dot(ref[...], w[0], preferred_element_type=F32)
        value = value + jnp.dot(ref[...], w[1], preferred_element_type=F32)
        fc_ref[i * CH : (i + 1) * CH, :] = value.astype(BF)


def survey(scalars, pair, other, mine, partner, w):
    whole = pl.BlockSpec(memory_space=pltpu.VMEM)
    far = pl.BlockSpec(memory_space=pltpu.HBM)
    return pl.pallas_call(
        survey_kernel,
        out_shape=[
            pltpu.VMEM((CH, 2 * CH), jnp.int32),
            jax.ShapeDtypeStruct((CH // GROUP + 8, 128), jnp.int32),
            pltpu.VMEM((2 * CH, PERIOD), BF),
            pltpu.VMEM((8, SAMPLES), jnp.int32),
        ],
        in_specs=[pl.BlockSpec(memory_space=pltpu.SMEM), far] + vmem(3) + [far],
        out_specs=[whole] * 4,
        scratch_shapes=[
            pltpu.VMEM((CH, CH), jnp.int32),
            pltpu.VMEM((2, SAMPLES, PERIOD), BF),
            pltpu.SemaphoreType.DMA((9,)),
        ],
        compiler_params=pltpu.CompilerParams(vmem_limit_bytes=LIMIT),
        cost_estimate=pl.CostEstimate(
            flops=2 * 2 * 2 * CH * SAMPLES * PERIOD, bytes_accessed=2 * 1024 * 1024, transcendentals=0
        ),
        name="survey",
    )(scalars, in_hbm(pair), other, mine, partner, in_hbm(w))


def prepare_kernel(
    scalars, low_ref, order_ref, pair_ref, other_ref, bins_ref, after_ref, hot_ref, pick_ref, tally_ref,
    words, ranks,
):
    core = scalars[0]
    columns = lax.broadcasted_iota(jnp.int32, (512, WIN), 1)
    lane = lax.broadcasted_iota(jnp.int32, (WIN, 128), 1)
    turned = jnp.concatenate([order_ref[...], jnp.zeros((120, 128), jnp.int32)], axis=0).T
    ranks[...] = turned.reshape(8, 2, 8, 128)
    half = ranks[:, core].reshape(64, 128)
    order = jnp.concatenate([half[:, a : a + 1] for a in range(8)], axis=0)
    tally = jnp.zeros((512, 128), F32)
    for i in range(2):
        step = core if i == 0 else 1 - core
        bins = jnp.concatenate([pair_ref[step], other_ref[step]], axis=1)
        lowest = jnp.min(jnp.min(bins, axis=0, keepdims=True), axis=1, keepdims=True)
        rel = bins - lowest
        place = rel % 32
        unit = jnp.left_shift(1, rel // 32 * 8)

        def body(j, carry):
            hit = jnp.where(place == j, unit, 0)
            hit = hit[:, :CH] + hit[:, CH:]
            pieces = [hit[q : q + 8] for q in range(0, CH, 8)]
            while len(pieces) > 1:
                pieces = [x + y for x, y in zip(pieces[::2], pieces[1::2])]
            words[pl.ds(pl.multiple_of(j * 8, 8), 8), :] = pieces[0]
            return carry

        lax.fori_loop(0, 32, body, 0, unroll=4)
        packed = words[...]
        pieces = []
        for q in range(WIN // 32):
            part = jnp.bitwise_and(jnp.right_shift(packed, 8 * q), 255)
            part = jnp.sum(part.reshape(32, 8, CH), axis=1)
            pieces.append(jnp.sum(part, axis=1, keepdims=True))
        counts = jnp.concatenate(pieces, axis=0)
        pick = jnp.where(order - lowest == columns, 1.0, 0.0).astype(BF)
        pick_ref[:, i * WIN : (i + 1) * WIN] = pick
        parts = jnp.where(lane == 2 * i, counts - counts % 256, 0)
        parts = parts + jnp.where(lane == 2 * i + 1, counts % 256, 0)
        tally = tally + jnp.dot(pick, parts.astype(F32).astype(BF), preferred_element_type=F32)
    tally_ref[...] = tally.astype(BF)

    offsets = lax.broadcasted_iota(jnp.int32, (SPAN, 2 * CH), 0)

    def mark(g, carry):
        rel = bins_ref[pl.ds(pl.multiple_of(g * GROUP, GROUP), GROUP), :] - low_ref[g, 0]
        for p in range(0, GROUP, 2):
            hot_ref[g, p * SPAN : (p + 2) * SPAN, :] = jnp.concatenate(
                [jnp.where(rel[q : q + 1, :] == offsets, 1.0, 0.0) for q in (p, p + 1)], axis=0
            ).astype(BF)
        return carry

    lax.fori_loop(0, CH // GROUP, mark, 0)


def prepare(scalars, lows, order, pair, other, bins, after):
    return pl.pallas_call(
        prepare_kernel,
        out_shape=[
            pltpu.VMEM((CH // GROUP, GROUP * SPAN, 2 * CH), BF),
            pltpu.VMEM((512, 2 * WIN), BF),
            pltpu.VMEM((512, 128), BF),
        ],
        in_specs=[pl.BlockSpec(memory_space=pltpu.SMEM)] * 2 + vmem(4) + [pl.BlockSpec(memory_space=pl.ANY)],
        out_specs=vmem(3),
        scratch_shapes=[pltpu.VMEM((32 * 8, CH), jnp.int32), pltpu.VMEM((8, 2, 8, 128), jnp.int32)],
        compiler_params=pltpu.CompilerParams(vmem_limit_bytes=LIMIT),
        cost_estimate=pl.CostEstimate(flops=10**9, bytes_accessed=2**20, transcendentals=0),
        name="prepare",
    )(scalars, lows, order, pair, other, bins, after)


def arrange_kernel(pick_ref, tally_ref, mine_ref, other_ref, out_ref):
    window = jnp.concatenate([mine_ref[...], other_ref[...]], axis=0)
    result = jnp.dot(pick_ref[...], window, preferred_element_type=F32)
    out_ref[:, :LAGS] = result.astype(BF)
    out_ref[:, LAGS:] = tally_ref[...]


def arrange(pick, tally, mine, other):
    return pl.pallas_call(
        arrange_kernel,
        out_shape=jax.ShapeDtypeStruct((512, LAGS + 128), BF),
        in_specs=vmem(4),
        out_specs=pl.BlockSpec(memory_space=pltpu.VMEM),
        compiler_params=pltpu.CompilerParams(vmem_limit_bytes=LIMIT),
        name="arrange",
    )(pick, tally, mine, other)


def finish_kernel(parts_ref, out_ref):
    value = jnp.sum(parts_ref[...].astype(F32).reshape(64, 8, LAGS + 128), axis=0)
    totals = jnp.sum(value[:, LAGS:], axis=1, keepdims=True)
    out_ref[...] = value[:, :LAGS] / jnp.sqrt(SAMPLES * totals)


def finish(parts):
    return pl.pallas_call(
        finish_kernel,
        out_shape=jax.ShapeDtypeStruct((8, LAGS), F32),
        in_specs=vmem(1),
        out_specs=pl.BlockSpec(memory_space=pltpu.VMEM),
        compiler_params=pltpu.CompilerParams(vmem_limit_bytes=LIMIT),
        name="finish",
    )(parts)


def shards(traces, band_group, filters, pair_bin, bin_order):
    both = ("src", "rcv")
    swap = [(i, i ^ 1) for i in range(32)]
    forward, back = transforms()
    w, back = jnp.asarray(forward), jnp.asarray(back)
    src, rcv = lax.axis_index("src"), lax.axis_index("rcv")
    core = rcv % 2
    y, z = (rcv // 2) % RING, rcv // 8
    root = jnp.logical_and(y == 2 * (src % 2), z % 2 == src // 2)
    keep = jnp.logical_or(jnp.logical_not(root), z // 2 == core)
    scalars = jnp.stack([core, root.astype(jnp.int32), keep.astype(jnp.int32)])

    across, up, along = plans()
    other_pair = lax.ppermute(pair_bin, "rcv", swap)
    filtered = prefilter(traces, band_group, filters)
    filtered, other_pair = lax.optimization_barrier((filtered, other_pair))
    got = lax.ppermute(filtered, both, across[0])
    partner = lax.ppermute(filtered, "rcv", swap)
    seed = jnp.where(core == 0, filtered, partner)
    got = got + lax.ppermute(seed, both, across[1])
    parts = [lax.ppermute(seed, both, plan) for plan in up]
    bins, table, fc, flag = survey(scalars, pair_bin, other_pair, filtered, partner, w)
    held = jnp.where(flag[0:1] == 1, seed, got)
    parts = parts + [lax.ppermute(held, both, plan) for plan in along]
    hot, pick, tally = prepare(
        scalars, table, bin_order.reshape(8, 128), pair_bin, other_pair, bins, held
    )

    window = correlate(scalars, table, held, parts, w, fc, bins, hot, back)
    other_window = lax.ppermute(window, "rcv", swap)
    payload = arrange(pick, tally, window, other_window)
    groups = [[2 * i + c for i in range(64)] for c in range(2)]
    arrived = lax.all_to_all(payload, both, 0, 0, tiled=True, axis_index_groups=groups)
    return finish(arrived)


def solution(mesh):
    in_specs = (P("rcv", None), P("rcv"), P(), P(None, "src", "rcv"), P())
    out_specs = P(("src", "rcv"), None)
    return jax.shard_map(shards, mesh=mesh, in_specs=in_specs, out_specs=out_specs, check_vma=False)
```

```python
import functools

import jax
import jax.numpy as jnp
import numpy as np
from jax import lax
from jax.experimental import pallas as pl
from jax.experimental.pallas import tpu as pltpu
from jax.sharding import PartitionSpec as P

LAGS = 512
SAMPLES = 512
TAPS = 32
FREQS = 384
PERIOD = 2 * FREQS
CH = 128
GROUP = 16
SPAN = 72
WIN = 128
LIMIT = 16 * 1024 * 1024
RING = 4
BF = jnp.bfloat16
F32 = jnp.float32


def split_bf16(matrix):
    high = matrix.astype(np.float32).astype(jnp.bfloat16)
    low = (matrix - high.astype(np.float64)).astype(np.float32).astype(jnp.bfloat16)
    return np.stack([high, low])


@functools.lru_cache(None)
def transforms():
    odd = 2 * np.arange(FREQS) + 1
    t = np.arange(SAMPLES)
    angle = np.pi / PERIOD * ((t[:, None] * odd[None, :]) % (2 * PERIOD))
    forward = np.stack([np.cos(angle), -np.sin(angle)], axis=1).reshape(SAMPLES, 2, -1, 128)
    forward = forward.transpose(0, 2, 1, 3).reshape(SAMPLES, PERIOD)
    lag = np.arange(LAGS) - LAGS // 2
    angle = np.pi / PERIOD * ((odd[:, None] * lag[None, :]) % (2 * PERIOD))
    back = np.stack([np.cos(angle), -np.sin(angle)], axis=0).reshape(2, -1, 128, LAGS)
    back = back.transpose(1, 0, 2, 3).reshape(PERIOD, LAGS) * (2.0 / PERIOD)
    return split_bf16(forward), split_bf16(back)


def device(src, z, y, core):
    return src * 32 + (z % RING) * 8 + (y % RING) * 2 + core


def owners():
    for s in range(4):
        for k in range(2):
            yield s, k, 2 * (s % 2), 2 * k + s // 2


def plans():
    up, across, along = [[], []], [], []
    for s, k, y, z in owners():
        up[k].append((device(s, z, y, 0), device(s, z + 2, y, k)))
        up[1 - k].append((device(s, z, y, 0), device(s, z - 1, y, k)))
        up[1].append((device(s, z, y, 1), device(s, z + 1, y, k)))
        across.append((device(s, z, y, 0), device(s, z, y + 2, k)))
        across.append((device(s, z, y, 1), device(s, z, y + 1, k)))
    for d in (2, 1, 3):
        plan = []
        for s, k, y, z in owners():
            for zz in range(0 if d == 3 else 1, RING):
                plan.append((device(s, z + zz, y, k), device(s, z + zz, y + d, k)))
        along.append(plan)
    return up, across, along


def in_hbm(value):
    return pltpu.with_memory_space_constraint(value, pltpu.HBM)


def vmem(n):
    return [pl.BlockSpec(memory_space=pltpu.VMEM)] * n


def prefilter_kernel(
    traces_hbm, band_hbm, filters_hbm, w_ref, out_ref, near_ref, pad_ref, traces_ref, band_ref, filters_ref, sems
):
    pairs = ((traces_hbm, traces_ref), (band_hbm, band_ref), (filters_hbm, filters_ref))
    inputs = [pltpu.make_async_copy(a, b, sems.at[8 + i]) for i, (a, b) in enumerate(pairs)]
    for copy in inputs:
        copy.start()
    copies = [
        pltpu.make_async_copy(
            w_ref.at[i, pl.ds(j, 128)], near_ref.at[i, pl.ds(j, 128)], sems.at[4 * i + j // 128]
        )
        for i in range(2)
        for j in range(0, SAMPLES, 128)
    ]
    for copy in copies:
        copy.start()
    pad_ref[0:TAPS, :] = jnp.zeros((TAPS, CH), F32)
    for copy in inputs:
        copy.wait()
    bands = filters_ref.shape[0]
    onehot = (lax.broadcasted_iota(jnp.int32, (bands, CH), 0) == band_ref[...]).astype(F32)
    taps = lax.dot_general(
        filters_ref[...],
        onehot,
        (((0,), (0,)), ((), ())),
        precision=lax.Precision.HIGHEST,
        preferred_element_type=F32,
    )
    pad_ref[TAPS:, :] = traces_ref[...].astype(F32).T
    rows = 128
    power = jnp.zeros((1, CH), F32)
    parts = []
    for start in range(0, SAMPLES, rows):
        total = jnp.zeros((rows, CH), F32)
        for k in range(TAPS):
            low = TAPS + start - k
            total = total + taps[k : k + 1, :] * pad_ref[low : low + rows, :]
        power = power + jnp.sum(total * total, axis=0, keepdims=True)
        parts.append(total)
    scale = lax.rsqrt(power * (1.0 / SAMPLES) + 1e-06)
    for i, total in enumerate(parts):
        out_ref[:, i * rows : (i + 1) * rows] = (total * scale).T.astype(BF)
    for copy in copies:
        copy.wait()


def prefilter(traces, band_group, filters, w):
    return pl.pallas_call(
        prefilter_kernel,
        out_shape=[pltpu.VMEM((CH, SAMPLES), BF), pltpu.VMEM((2, SAMPLES, PERIOD), BF)],
        in_specs=[pl.BlockSpec(memory_space=pltpu.HBM)] * 4,
        out_specs=vmem(2),
        scratch_shapes=[
            pltpu.VMEM((TAPS + SAMPLES, CH), F32),
            pltpu.VMEM((CH, SAMPLES), BF),
            pltpu.VMEM((1, CH), jnp.int32),
            pltpu.VMEM(filters.shape, F32),
            pltpu.SemaphoreType.DMA((11,)),
        ],
        compiler_params=pltpu.CompilerParams(vmem_limit_bytes=LIMIT),
        name="prefilter",
    )(in_hbm(traces), in_hbm(band_group.reshape(1, CH)), in_hbm(filters), in_hbm(w))


def correlate_kernel(
    low_ref, held_ref, r0, r1, r2, r3, w_ref, fc_ref, bins_ref, hot_ref, back_ref, out_ref,
    fs, total, wide,
):
    block = held_ref[...] + ((r0[...] + r1[...]) + (r2[...] + r3[...]))
    fs[...] = jnp.dot(block, w_ref[0], preferred_element_type=F32) + jnp.dot(
        block, w_ref[1], preferred_element_type=F32
    )
    total[...] = jnp.zeros_like(total)
    n_groups = CH // GROUP

    def spread(hot, j):
        return jnp.dot(hot, fc_ref[:, j * 256 : (j + 1) * 256], preferred_element_type=F32)

    def gather(g, j, span, buffer):
        first = pl.multiple_of(g * GROUP, GROUP)
        low = low_ref[g, 0]
        shift = low % 8
        start = pl.multiple_of(low - shift, 8)
        room = jnp.zeros((8, 128), F32)
        re, im = slice(j * 256, j * 256 + 128), slice(j * 256 + 128, (j + 1) * 256)
        fr, fi = fs[pl.ds(first, GROUP), re], fs[pl.ds(first, GROUP), im]
        sum_re = jnp.zeros((span, 128), F32)
        sum_im = jnp.zeros((span, 128), F32)
        for p in range(GROUP):
            rows = slice(p * span, (p + 1) * span)
            gr, gi = buffer[rows, 0:128], buffer[rows, 128:256]
            a, b = fr[p : p + 1, :], fi[p : p + 1, :]
            sum_re = sum_re + (a * gr + b * gi)
            sum_im = sum_im + (a * gi - b * gr)
        for part, value in ((re, sum_re), (im, sum_im)):
            moved = pltpu.roll(jnp.concatenate([value, room], axis=0), shift, 0)
            total[pl.ds(start, span + 8), part] += moved

    fits = low_ref[n_groups, 0] == 1

    @pl.when(fits)
    def _():
        def body(g, carry):
            for j in range(3):
                gather(g, j, SPAN, spread(hot_ref[g], j))
            return carry

        lax.fori_loop(0, n_groups, body, 0, unroll=2)

    @pl.when(jnp.logical_not(fits))
    def _():
        offsets = lax.broadcasted_iota(jnp.int32, (WIN, 2 * CH), 0)

        def body(g, carry):
            rel = bins_ref[pl.ds(pl.multiple_of(g * GROUP, GROUP), GROUP), :]
            for p in range(GROUP):
                row = jnp.where(rel[p : p + 1, :] == offsets, 1.0, 0.0)
                wide[p * WIN : (p + 1) * WIN, :] = row.astype(BF)
            for j in range(3):
                gather(g, j, WIN, spread(wide[...], j))
            return carry

        lax.fori_loop(0, n_groups, body, 0)

    for start in range(0, WIN, 128):
        value = total[start : start + 128, :]
        high = value.astype(BF)
        low = (value - high.astype(F32)).astype(BF)
        value = (
            jnp.dot(high, back_ref[0], preferred_element_type=F32)
            + jnp.dot(low, back_ref[0], preferred_element_type=F32)
            + jnp.dot(high, back_ref[1], preferred_element_type=F32)
        )
        out_ref[start : start + 128, :] = value.astype(BF)


def correlate(lows, held, parts, w, fc, bins, hot, back):
    return pl.pallas_call(
        correlate_kernel,
        out_shape=jax.ShapeDtypeStruct((WIN, LAGS), BF),
        in_specs=[pl.BlockSpec(memory_space=pltpu.SMEM)] + vmem(10),
        out_specs=pl.BlockSpec(memory_space=pltpu.VMEM),
        scratch_shapes=[
            pltpu.VMEM((CH, PERIOD), F32),
            pltpu.VMEM((2 * WIN, PERIOD), F32),
            pltpu.VMEM((GROUP * WIN, 2 * CH), BF),
        ],
        compiler_params=pltpu.CompilerParams(vmem_limit_bytes=LIMIT),
        cost_estimate=pl.CostEstimate(
            flops=2 * 128 * SPAN * 256 * PERIOD, bytes_accessed=6 * 1024 * 1024, transcendentals=0
        ),
        name="correlate",
    )(lows, held, *parts, w, fc, bins, hot, back)


def survey_kernel(
    scalars, pair_ref, other_ref, mine_ref, partner_ref, w_ref, bins_ref, table_ref, fc_ref, flag_ref, raw, sem
):
    core = scalars[0]
    copy = pltpu.make_async_copy(pair_ref.at[core], raw, sem)
    copy.start()
    flag_ref[...] = jnp.full(flag_ref.shape, scalars[1], jnp.int32)
    for i, ref in enumerate((mine_ref, partner_ref)):
        value = jnp.dot(ref[...], w_ref[0], preferred_element_type=F32)
        value = value + jnp.dot(ref[...], w_ref[1], preferred_element_type=F32)
        fc_ref[i * CH : (i + 1) * CH, :] = value.astype(BF)
    copy.wait()
    bins = jnp.concatenate([raw[...], other_ref[core]], axis=1)
    lowest = jnp.min(jnp.min(bins, axis=0, keepdims=True), axis=1, keepdims=True)
    rel = bins - lowest
    bins_ref[...] = rel
    n_groups = CH // GROUP
    grouped = rel.reshape(n_groups, GROUP, 2 * CH)
    low = jnp.min(jnp.min(grouped, axis=1), axis=1, keepdims=True)
    high = jnp.max(jnp.max(grouped, axis=1), axis=1, keepdims=True)
    widest = jnp.max(high - low, axis=0, keepdims=True)
    fits = (widest < SPAN).astype(jnp.int32)
    low = jnp.minimum(low * fits, WIN)
    table_ref[0:n_groups, :] = jnp.broadcast_to(low, (n_groups, 128))
    table_ref[n_groups:, :] = jnp.broadcast_to(fits, (8, 128))

def tally_of(rel, words):
    place = rel % 32
    unit = jnp.left_shift(1, rel // 32 * 8)

    def body(j, carry):
        hit = jnp.where(place == j, unit, 0)
        hit = hit[:, :CH] + hit[:, CH:]
        pieces = [hit[q : q + 8] for q in range(0, CH, 8)]
        while len(pieces) > 1:
            pieces = [x + y for x, y in zip(pieces[::2], pieces[1::2])]
        words[pl.ds(pl.multiple_of(j * 8, 8), 8), :] = pieces[0]
        return carry

    lax.fori_loop(0, 32, body, 0, unroll=4)
    packed = words[...]
    pieces = []
    for q in range(WIN // 32):
        part = jnp.bitwise_and(jnp.right_shift(packed, 8 * q), 255)
        part = jnp.sum(part.reshape(32, 8, CH), axis=1)
        pieces.append(jnp.sum(part, axis=1, keepdims=True))
    return jnp.concatenate(pieces, axis=0)


def survey(scalars, pair, other, mine, partner, w):
    whole = pl.BlockSpec(memory_space=pltpu.VMEM)
    far = pl.BlockSpec(memory_space=pltpu.HBM)
    return pl.pallas_call(
        survey_kernel,
        out_shape=[
            pltpu.VMEM((CH, 2 * CH), jnp.int32),
            jax.ShapeDtypeStruct((CH // GROUP + 8, 128), jnp.int32),
            pltpu.VMEM((2 * CH, PERIOD), BF),
            pltpu.VMEM((8, SAMPLES), jnp.int32),
        ],
        in_specs=[pl.BlockSpec(memory_space=pltpu.SMEM), far] + vmem(4),
        out_specs=[whole] * 4,
        scratch_shapes=[
            pltpu.VMEM((CH, CH), jnp.int32),
            pltpu.SemaphoreType.DMA,
        ],
        compiler_params=pltpu.CompilerParams(vmem_limit_bytes=LIMIT),
        cost_estimate=pl.CostEstimate(
            flops=2 * 2 * 2 * CH * SAMPLES * PERIOD, bytes_accessed=2 * 1024 * 1024, transcendentals=0
        ),
        name="survey",
    )(scalars, in_hbm(pair), other, mine, partner, w)


def prepare_kernel(
    scalars, low_ref, order_ref, pair_ref, other_ref, bins_ref, after_ref, hot_ref, pick_ref, tally_ref,
    ranks, words,
):
    core = scalars[0]
    columns = lax.broadcasted_iota(jnp.int32, (512, WIN), 1)
    lane = lax.broadcasted_iota(jnp.int32, (WIN, 128), 1)
    turned = jnp.concatenate([order_ref[...], jnp.zeros((120, 128), jnp.int32)], axis=0).T
    ranks[...] = turned.reshape(8, 2, 8, 128)
    half = ranks[:, core].reshape(64, 128)
    order = jnp.concatenate([half[:, a : a + 1] for a in range(8)], axis=0)
    tally = jnp.zeros((512, 128), F32)
    for i in range(2):
        step = core if i == 0 else 1 - core
        bins = jnp.concatenate([pair_ref[step], other_ref[step]], axis=1)
        lowest = jnp.min(jnp.min(bins, axis=0, keepdims=True), axis=1, keepdims=True)
        counts = tally_of(bins - lowest, words)
        pick = jnp.where(order - lowest == columns, 1.0, 0.0).astype(BF)
        pick_ref[:, i * WIN : (i + 1) * WIN] = pick
        parts = jnp.where(lane == 2 * i, counts - counts % 256, 0)
        parts = parts + jnp.where(lane == 2 * i + 1, counts % 256, 0)
        tally = tally + jnp.dot(pick, parts.astype(F32).astype(BF), preferred_element_type=F32)
    tally_ref[...] = tally.astype(BF)

    offsets = lax.broadcasted_iota(jnp.int32, (SPAN, 2 * CH), 0)

    def mark(g, carry):
        rel = bins_ref[pl.ds(pl.multiple_of(g * GROUP, GROUP), GROUP), :] - low_ref[g, 0]
        for p in range(0, GROUP, 2):
            hot_ref[g, p * SPAN : (p + 2) * SPAN, :] = jnp.concatenate(
                [jnp.where(rel[q : q + 1, :] == offsets, 1.0, 0.0) for q in (p, p + 1)], axis=0
            ).astype(BF)
        return carry

    lax.fori_loop(0, CH // GROUP, mark, 0)


def prepare(scalars, lows, order, pair, other, bins, after):
    return pl.pallas_call(
        prepare_kernel,
        out_shape=[
            pltpu.VMEM((CH // GROUP, GROUP * SPAN, 2 * CH), BF),
            pltpu.VMEM((512, 2 * WIN), BF),
            pltpu.VMEM((512, 128), BF),
        ],
        in_specs=[pl.BlockSpec(memory_space=pltpu.SMEM)] * 2 + vmem(4) + [pl.BlockSpec(memory_space=pl.ANY)],
        out_specs=vmem(3),
        scratch_shapes=[pltpu.VMEM((8, 2, 8, 128), jnp.int32), pltpu.VMEM((32 * 8, CH), jnp.int32)],
        compiler_params=pltpu.CompilerParams(vmem_limit_bytes=LIMIT),
        cost_estimate=pl.CostEstimate(flops=10**9, bytes_accessed=2**20, transcendentals=0),
        name="prepare",
    )(scalars, lows, order, pair, other, bins, after)


def arrange_kernel(pick_ref, tally_ref, mine_ref, other_ref, out_ref):
    window = jnp.concatenate([mine_ref[...], other_ref[...]], axis=0)
    result = jnp.dot(pick_ref[...], window, preferred_element_type=F32)
    out_ref[:, :LAGS] = result.astype(BF)
    out_ref[:, LAGS:] = tally_ref[...]


def arrange(pick, tally, mine, other):
    return pl.pallas_call(
        arrange_kernel,
        out_shape=jax.ShapeDtypeStruct((512, LAGS + 128), BF),
        in_specs=vmem(4),
        out_specs=pl.BlockSpec(memory_space=pltpu.VMEM),
        compiler_params=pltpu.CompilerParams(vmem_limit_bytes=LIMIT),
        name="arrange",
    )(pick, tally, mine, other)


def finish_kernel(parts_ref, out_ref):
    value = jnp.sum(parts_ref[...].astype(F32).reshape(64, 8, LAGS + 128), axis=0)
    totals = jnp.sum(value[:, LAGS:], axis=1, keepdims=True)
    out_ref[...] = value[:, :LAGS] / jnp.sqrt(SAMPLES * totals)


def finish(parts):
    return pl.pallas_call(
        finish_kernel,
        out_shape=jax.ShapeDtypeStruct((8, LAGS), F32),
        in_specs=vmem(1),
        out_specs=pl.BlockSpec(memory_space=pltpu.VMEM),
        compiler_params=pltpu.CompilerParams(vmem_limit_bytes=LIMIT),
        name="finish",
    )(parts)


def shards(traces, band_group, filters, pair_bin, bin_order):
    both = ("src", "rcv")
    swap = [(i, i ^ 1) for i in range(32)]
    forward, back = transforms()
    w, back = jnp.asarray(forward), jnp.asarray(back)
    src, rcv = lax.axis_index("src"), lax.axis_index("rcv")
    core = rcv % 2
    y, z = (rcv // 2) % RING, rcv // 8
    owner = jnp.logical_and(y == 2 * (src % 2), z == 2 * core + src // 2)
    scalars = jnp.stack([core, owner.astype(jnp.int32)])

    up, across, along = plans()
    other_pair = lax.ppermute(pair_bin, "rcv", swap)
    filtered, w = prefilter(traces, band_group, filters, w)
    filtered, other_pair = lax.optimization_barrier((filtered, other_pair))
    got = lax.ppermute(filtered, both, up[0])
    partner = lax.ppermute(filtered, "rcv", swap)
    seed = jnp.where(core == 0, filtered, partner)
    got = got + lax.ppermute(seed, both, up[1])
    parts = [lax.ppermute(seed, both, across)]
    bins, table, fc, flag = survey(scalars, pair_bin, other_pair, filtered, partner, w)
    held = jnp.where(flag[0:1] == 1, seed, got)
    parts = parts + [lax.ppermute(held, both, plan) for plan in along]
    hot, pick, tally = prepare(
        scalars, table, bin_order.reshape(8, 128), pair_bin, other_pair, bins, held
    )

    window = correlate(table, held, parts, w, fc, bins, hot, back)
    other_window = lax.ppermute(window, "rcv", swap)
    payload = arrange(pick, tally, window, other_window)
    groups = [[2 * i + c for i in range(64)] for c in range(2)]
    arrived = lax.all_to_all(payload, both, 0, 0, tiled=True, axis_index_groups=groups)
    return finish(arrived)


def solution(mesh):
    in_specs = (P("rcv", None), P("rcv"), P(), P(None, "src", "rcv"), P())
    out_specs = P(("src", "rcv"), None)
    return jax.shard_map(shards, mesh=mesh, in_specs=in_specs, out_specs=out_specs, check_vma=False)
```

```python
import functools

import jax
import jax.numpy as jnp
import numpy as np
from jax import lax
from jax.experimental import pallas as pl
from jax.experimental.pallas import tpu as pltpu
from jax.sharding import PartitionSpec as P

LAGS = 512
SAMPLES = 512
TAPS = 32
FREQS = 384
PERIOD = 2 * FREQS
CH = 128
GROUP = 16
SPAN = 72
WIN = 128
LIMIT = 16 * 1024 * 1024
RING = 4
BF = jnp.bfloat16
F32 = jnp.float32


def split_bf16(matrix):
    high = matrix.astype(np.float32).astype(jnp.bfloat16)
    low = (matrix - high.astype(np.float64)).astype(np.float32).astype(jnp.bfloat16)
    return np.stack([high, low])


@functools.lru_cache(None)
def transforms():
    odd = 2 * np.arange(FREQS) + 1
    t = np.arange(SAMPLES)
    angle = np.pi / PERIOD * ((t[:, None] * odd[None, :]) % (2 * PERIOD))
    forward = np.stack([np.cos(angle), -np.sin(angle)], axis=1).reshape(SAMPLES, 2, -1, 128)
    forward = forward.transpose(0, 2, 1, 3).reshape(SAMPLES, PERIOD)
    lag = np.arange(LAGS) - LAGS // 2
    angle = np.pi / PERIOD * ((odd[:, None] * lag[None, :]) % (2 * PERIOD))
    back = np.stack([np.cos(angle), -np.sin(angle)], axis=0).reshape(2, -1, 128, LAGS)
    back = back.transpose(1, 0, 2, 3).reshape(PERIOD, LAGS) * (2.0 / PERIOD)
    return split_bf16(forward), split_bf16(back)


def device(src, z, y, core):
    return src * 32 + (z % RING) * 8 + (y % RING) * 2 + core


def owners():
    for s in range(4):
        for k in range(2):
            yield s, k, 2 * (s % 2), 2 * k + s // 2


def plans():
    first, side, along = [[], []], [], [[], [], []]
    for s, k, y, z in owners():

        def chip(own, across, core, s=s, k=k, y=y, z=z):
            return device(s, z + (across if k == 0 else own), y + (own if k == 0 else across), core)

        first[0].append((chip(0, 0, 0), chip(-1, 0, k)))
        first[1].append((chip(0, 0, 0), chip(2, 0, k)))
        first[1].append((chip(0, 0, 1), chip(1, 0, k)))
        side.append((chip(0, 0, 0), chip(0, 2, k)))
        side.append((chip(0, 0, 1), chip(0, 1, k)))
        for plan, d in zip(along, (2, 1, 3)):
            plan.extend((chip(i, 0, k), chip(i, d, k)) for i in range(0 if d == 3 else 1, RING))
    return first, side, along


def in_hbm(value):
    return pltpu.with_memory_space_constraint(value, pltpu.HBM)


def vmem(n):
    return [pl.BlockSpec(memory_space=pltpu.VMEM)] * n


def prefilter_kernel(
    traces_hbm, band_hbm, filters_hbm, w_ref, out_ref, near_ref, pad_ref, traces_ref, band_ref, filters_ref, sems
):
    pairs = ((traces_hbm, traces_ref), (band_hbm, band_ref), (filters_hbm, filters_ref))
    inputs = [pltpu.make_async_copy(a, b, sems.at[8 + i]) for i, (a, b) in enumerate(pairs)]
    for copy in inputs:
        copy.start()
    copies = [
        pltpu.make_async_copy(
            w_ref.at[i, pl.ds(j, 128)], near_ref.at[i, pl.ds(j, 128)], sems.at[4 * i + j // 128]
        )
        for i in range(2)
        for j in range(0, SAMPLES, 128)
    ]
    for copy in copies:
        copy.start()
    pad_ref[0:TAPS, :] = jnp.zeros((TAPS, CH), F32)
    for copy in inputs:
        copy.wait()
    bands = filters_ref.shape[0]
    onehot = (lax.broadcasted_iota(jnp.int32, (bands, CH), 0) == band_ref[...]).astype(F32)
    taps = lax.dot_general(
        filters_ref[...],
        onehot,
        (((0,), (0,)), ((), ())),
        precision=lax.Precision.HIGHEST,
        preferred_element_type=F32,
    )
    pad_ref[TAPS:, :] = traces_ref[...].astype(F32).T
    rows = 128
    power = jnp.zeros((1, CH), F32)
    parts = []
    for start in range(0, SAMPLES, rows):
        total = jnp.zeros((rows, CH), F32)
        for k in range(TAPS):
            low = TAPS + start - k
            total = total + taps[k : k + 1, :] * pad_ref[low : low + rows, :]
        power = power + jnp.sum(total * total, axis=0, keepdims=True)
        parts.append(total)
    scale = lax.rsqrt(power * (1.0 / SAMPLES) + 1e-06)
    for i, total in enumerate(parts):
        out_ref[:, i * rows : (i + 1) * rows] = (total * scale).T.astype(BF)
    for copy in copies:
        copy.wait()


def prefilter(traces, band_group, filters, w):
    return pl.pallas_call(
        prefilter_kernel,
        out_shape=[pltpu.VMEM((CH, SAMPLES), BF), pltpu.VMEM((2, SAMPLES, PERIOD), BF)],
        in_specs=[pl.BlockSpec(memory_space=pltpu.HBM)] * 4,
        out_specs=vmem(2),
        scratch_shapes=[
            pltpu.VMEM((TAPS + SAMPLES, CH), F32),
            pltpu.VMEM((CH, SAMPLES), BF),
            pltpu.VMEM((1, CH), jnp.int32),
            pltpu.VMEM(filters.shape, F32),
            pltpu.SemaphoreType.DMA((11,)),
        ],
        compiler_params=pltpu.CompilerParams(vmem_limit_bytes=LIMIT),
        name="prefilter",
    )(in_hbm(traces), in_hbm(band_group.reshape(1, CH)), in_hbm(filters), in_hbm(w))


def correlate_kernel(
    low_ref, held_ref, r0, r1, r2, r3, w_ref, fc_ref, bins_ref, hot_ref, pieces_ref, back_ref, out_ref,
    fs, total, wide,
):
    block = held_ref[...] + ((r0[...] + r1[...]) + (r2[...] + r3[...]))
    fs[...] = jnp.dot(block, w_ref[0], preferred_element_type=F32) + jnp.dot(
        block, w_ref[1], preferred_element_type=F32
    )
    total[...] = jnp.zeros_like(total)
    n_groups = CH // GROUP

    def spread(hot, j):
        return jnp.dot(hot, fc_ref[:, j * 256 : (j + 1) * 256], preferred_element_type=F32)

    def gather(g, j, span, buffer):
        first = pl.multiple_of(g * GROUP, GROUP)
        low = low_ref[g, 0]
        shift = low % 8
        start = pl.multiple_of(low - shift, 8)
        room = jnp.zeros((8, 128), F32)
        re, im = slice(j * 256, j * 256 + 128), slice(j * 256 + 128, (j + 1) * 256)
        fr, fi = fs[pl.ds(first, GROUP), re], fs[pl.ds(first, GROUP), im]
        sum_re = jnp.zeros((span, 128), F32)
        sum_im = jnp.zeros((span, 128), F32)
        for p in range(GROUP):
            rows = slice(p * span, (p + 1) * span)
            gr, gi = buffer[rows, 0:128], buffer[rows, 128:256]
            a, b = fr[p : p + 1, :], fi[p : p + 1, :]
            sum_re = sum_re + (a * gr + b * gi)
            sum_im = sum_im + (a * gi - b * gr)
        for part, value in ((re, sum_re), (im, sum_im)):
            moved = pltpu.roll(jnp.concatenate([value, room], axis=0), shift, 0)
            total[pl.ds(start, span + 8), part] += moved

    fits = low_ref[n_groups, 0] == 1

    @pl.when(fits)
    def _():
        def body(g, carry):
            for j in range(3):
                gather(g, j, SPAN, spread(hot_ref[g], j))
            return carry

        lax.fori_loop(0, n_groups, body, 0, unroll=2)

    @pl.when(jnp.logical_not(fits))
    def _():
        offsets = lax.broadcasted_iota(jnp.int32, (WIN, 2 * CH), 0)

        def body(g, carry):
            rel = bins_ref[pl.ds(pl.multiple_of(g * GROUP, GROUP), GROUP), :]
            for p in range(GROUP):
                row = jnp.where(rel[p : p + 1, :] == offsets, 1.0, 0.0)
                wide[p * WIN : (p + 1) * WIN, :] = row.astype(BF)
            for j in range(3):
                gather(g, j, WIN, spread(wide[...], j))
            return carry

        lax.fori_loop(0, n_groups, body, 0)

    for start in range(0, WIN, 128):
        value = total[start : start + 128, :]
        high = value.astype(BF)
        low = (value - high.astype(F32)).astype(BF)
        value = (
            jnp.dot(high, back_ref[0], preferred_element_type=F32)
            + jnp.dot(low, back_ref[0], preferred_element_type=F32)
            + jnp.dot(high, back_ref[1], preferred_element_type=F32)
        )
        out_ref[start : start + 128, :LAGS] = value.astype(BF)
    out_ref[:, LAGS:] = pieces_ref[...]


def correlate(lows, held, parts, w, fc, bins, hot, pieces, back):
    return pl.pallas_call(
        correlate_kernel,
        out_shape=jax.ShapeDtypeStruct((WIN, LAGS + 128), BF),
        in_specs=[pl.BlockSpec(memory_space=pltpu.SMEM)] + vmem(11),
        out_specs=pl.BlockSpec(memory_space=pltpu.VMEM),
        scratch_shapes=[
            pltpu.VMEM((CH, PERIOD), F32),
            pltpu.VMEM((2 * WIN, PERIOD), F32),
            pltpu.VMEM((GROUP * WIN, 2 * CH), BF),
        ],
        compiler_params=pltpu.CompilerParams(vmem_limit_bytes=LIMIT),
        cost_estimate=pl.CostEstimate(
            flops=2 * 128 * SPAN * 256 * PERIOD, bytes_accessed=6 * 1024 * 1024, transcendentals=0
        ),
        name="correlate",
    )(lows, held, *parts, w, fc, bins, hot, pieces, back)


def survey_kernel(
    scalars, pair_ref, other_ref, mine_ref, partner_ref, w_ref, bins_ref, table_ref, fc_ref, flag_ref, pieces_ref,
    raw, words, sem,
):
    core = scalars[0]
    copy = pltpu.make_async_copy(pair_ref.at[core], raw, sem)
    copy.start()
    flag_ref[...] = jnp.full(flag_ref.shape, scalars[1], jnp.int32)
    for i, ref in enumerate((mine_ref, partner_ref)):
        value = jnp.dot(ref[...], w_ref[0], preferred_element_type=F32)
        value = value + jnp.dot(ref[...], w_ref[1], preferred_element_type=F32)
        fc_ref[i * CH : (i + 1) * CH, :] = value.astype(BF)
    copy.wait()
    bins = jnp.concatenate([raw[...], other_ref[core]], axis=1)
    lowest = jnp.min(jnp.min(bins, axis=0, keepdims=True), axis=1, keepdims=True)
    rel = bins - lowest
    bins_ref[...] = rel
    n_groups = CH // GROUP
    grouped = rel.reshape(n_groups, GROUP, 2 * CH)
    low = jnp.min(jnp.min(grouped, axis=1), axis=1, keepdims=True)
    high = jnp.max(jnp.max(grouped, axis=1), axis=1, keepdims=True)
    widest = jnp.max(high - low, axis=0, keepdims=True)
    fits = (widest < SPAN).astype(jnp.int32)
    low = jnp.minimum(low * fits, WIN)
    table_ref[0:n_groups, :] = jnp.broadcast_to(low, (n_groups, 128))
    table_ref[n_groups:, :] = jnp.broadcast_to(fits, (8, 128))
    counts = tally_of(rel, words)
    lane = lax.broadcasted_iota(jnp.int32, (WIN, 128), 1) - 2 * core
    pieces = jnp.where(lane == 0, counts - counts % 256, 0) + jnp.where(lane == 1, counts % 256, 0)
    pieces_ref[...] = pieces.astype(F32).astype(BF)

def tally_of(rel, words):
    place = rel % 32
    unit = jnp.left_shift(1, rel // 32 * 8)

    def body(j, carry):
        hit = jnp.where(place == j, unit, 0)
        hit = hit[:, :CH] + hit[:, CH:]
        pieces = [hit[q : q + 8] for q in range(0, CH, 8)]
        while len(pieces) > 1:
            pieces = [x + y for x, y in zip(pieces[::2], pieces[1::2])]
        words[pl.ds(pl.multiple_of(j * 8, 8), 8), :] = pieces[0]
        return carry

    lax.fori_loop(0, 32, body, 0, unroll=4)
    packed = words[...]
    pieces = []
    for q in range(WIN // 32):
        part = jnp.bitwise_and(jnp.right_shift(packed, 8 * q), 255)
        part = jnp.sum(part.reshape(32, 8, CH), axis=1)
        pieces.append(jnp.sum(part, axis=1, keepdims=True))
    return jnp.concatenate(pieces, axis=0)


def survey(scalars, pair, other, mine, partner, w):
    whole = pl.BlockSpec(memory_space=pltpu.VMEM)
    far = pl.BlockSpec(memory_space=pltpu.HBM)
    return pl.pallas_call(
        survey_kernel,
        out_shape=[
            pltpu.VMEM((CH, 2 * CH), jnp.int32),
            jax.ShapeDtypeStruct((CH // GROUP + 8, 128), jnp.int32),
            pltpu.VMEM((2 * CH, PERIOD), BF),
            pltpu.VMEM((8, SAMPLES), jnp.int32),
            pltpu.VMEM((WIN, 128), BF),
        ],
        in_specs=[pl.BlockSpec(memory_space=pltpu.SMEM), far] + vmem(4),
        out_specs=[whole] * 5,
        scratch_shapes=[
            pltpu.VMEM((CH, CH), jnp.int32),
            pltpu.VMEM((32 * 8, CH), jnp.int32),
            pltpu.SemaphoreType.DMA,
        ],
        compiler_params=pltpu.CompilerParams(vmem_limit_bytes=LIMIT),
        cost_estimate=pl.CostEstimate(
            flops=2 * 2 * 2 * CH * SAMPLES * PERIOD, bytes_accessed=2 * 1024 * 1024, transcendentals=0
        ),
        name="survey",
    )(scalars, in_hbm(pair), other, mine, partner, w)


def prepare_kernel(
    scalars, low_ref, order_ref, pair_ref, other_ref, bins_ref, after_ref, hot_ref, pick_ref,
    ranks,
):
    core = scalars[0]
    columns = lax.broadcasted_iota(jnp.int32, (512, WIN), 1)
    turned = jnp.concatenate([order_ref[...], jnp.zeros((120, 128), jnp.int32)], axis=0).T
    ranks[...] = turned.reshape(8, 2, 8, 128)
    half = ranks[:, core].reshape(64, 128)
    order = jnp.concatenate([half[:, a : a + 1] for a in range(8)], axis=0)
    for i in range(2):
        step = core if i == 0 else 1 - core
        bins = jnp.concatenate([pair_ref[step], other_ref[step]], axis=1)
        lowest = jnp.min(jnp.min(bins, axis=0, keepdims=True), axis=1, keepdims=True)
        pick = jnp.where(order - lowest == columns, 1.0, 0.0).astype(BF)
        pick_ref[:, i * WIN : (i + 1) * WIN] = pick

    offsets = lax.broadcasted_iota(jnp.int32, (SPAN, 2 * CH), 0)

    def mark(g, carry):
        rel = bins_ref[pl.ds(pl.multiple_of(g * GROUP, GROUP), GROUP), :] - low_ref[g, 0]
        for p in range(0, GROUP, 2):
            hot_ref[g, p * SPAN : (p + 2) * SPAN, :] = jnp.concatenate(
                [jnp.where(rel[q : q + 1, :] == offsets, 1.0, 0.0) for q in (p, p + 1)], axis=0
            ).astype(BF)
        return carry

    lax.fori_loop(0, CH // GROUP, mark, 0)


def prepare(scalars, lows, order, pair, other, bins, after):
    return pl.pallas_call(
        prepare_kernel,
        out_shape=[
            pltpu.VMEM((CH // GROUP, GROUP * SPAN, 2 * CH), BF),
            pltpu.VMEM((512, 2 * WIN), BF),
        ],
        in_specs=[pl.BlockSpec(memory_space=pltpu.SMEM)] * 2 + vmem(4) + [pl.BlockSpec(memory_space=pl.ANY)],
        out_specs=vmem(2),
        scratch_shapes=[pltpu.VMEM((8, 2, 8, 128), jnp.int32)],
        compiler_params=pltpu.CompilerParams(vmem_limit_bytes=LIMIT),
        cost_estimate=pl.CostEstimate(flops=10**9, bytes_accessed=2**20, transcendentals=0),
        name="prepare",
    )(scalars, lows, order, pair, other, bins, after)


def arrange_kernel(pick_ref, mine_ref, other_ref, out_ref):
    window = jnp.concatenate([mine_ref[...], other_ref[...]], axis=0)
    out_ref[...] = jnp.dot(pick_ref[...], window, preferred_element_type=F32).astype(BF)


def arrange(pick, mine, other):
    return pl.pallas_call(
        arrange_kernel,
        out_shape=jax.ShapeDtypeStruct((512, LAGS + 128), BF),
        in_specs=vmem(3),
        out_specs=pl.BlockSpec(memory_space=pltpu.VMEM),
        compiler_params=pltpu.CompilerParams(vmem_limit_bytes=LIMIT),
        name="arrange",
    )(pick, mine, other)


def finish_kernel(parts_ref, out_ref):
    value = jnp.sum(parts_ref[...].astype(F32).reshape(64, 8, LAGS + 128), axis=0)
    totals = jnp.sum(value[:, LAGS:], axis=1, keepdims=True)
    out_ref[...] = value[:, :LAGS] / jnp.sqrt(SAMPLES * totals)


def finish(parts):
    return pl.pallas_call(
        finish_kernel,
        out_shape=jax.ShapeDtypeStruct((8, LAGS), F32),
        in_specs=vmem(1),
        out_specs=pl.BlockSpec(memory_space=pltpu.VMEM),
        compiler_params=pltpu.CompilerParams(vmem_limit_bytes=LIMIT),
        name="finish",
    )(parts)


def shards(traces, band_group, filters, pair_bin, bin_order):
    both = ("src", "rcv")
    swap = [(i, i ^ 1) for i in range(32)]
    forward, back = transforms()
    w, back = jnp.asarray(forward), jnp.asarray(back)
    src, rcv = lax.axis_index("src"), lax.axis_index("rcv")
    core = rcv % 2
    y, z = (rcv // 2) % RING, rcv // 8
    owner = jnp.logical_and(y == 2 * (src % 2), z == 2 * core + src // 2)
    scalars = jnp.stack([core, owner.astype(jnp.int32)])

    first, side, along = plans()
    other_pair = lax.ppermute(pair_bin, "rcv", swap)
    filtered, w = prefilter(traces, band_group, filters, w)
    filtered, other_pair = lax.optimization_barrier((filtered, other_pair))
    got = lax.ppermute(filtered, both, first[0])
    partner = lax.ppermute(filtered, "rcv", swap)
    seed = jnp.where(core == 0, filtered, partner)
    got = got + lax.ppermute(seed, both, first[1])
    parts = [lax.ppermute(seed, both, side)]
    bins, table, fc, flag, pieces = survey(scalars, pair_bin, other_pair, filtered, partner, w)
    held = jnp.where(flag[0:1] == 1, seed, got)
    parts = parts + [lax.ppermute(held, both, plan) for plan in along]
    hot, pick = prepare(
        scalars, table, bin_order.reshape(8, 128), pair_bin, other_pair, bins, held
    )

    window = correlate(table, held, parts, w, fc, bins, hot, pieces, back)
    other_window = lax.ppermute(window, "rcv", swap)
    payload = arrange(pick, window, other_window)
    groups = [[2 * i + c for i in range(64)] for c in range(2)]
    arrived = lax.all_to_all(payload, both, 0, 0, tiled=True, axis_index_groups=groups)
    return finish(arrived)


def solution(mesh):
    in_specs = (P("rcv", None), P("rcv"), P(), P(None, "src", "rcv"), P())
    out_specs = P(("src", "rcv"), None)
    return jax.shard_map(shards, mesh=mesh, in_specs=in_specs, out_specs=out_specs, check_vma=False)
```

```python
import functools

import jax
import jax.numpy as jnp
import numpy as np
from jax import lax
from jax.experimental import pallas as pl
from jax.experimental.pallas import tpu as pltpu
from jax.sharding import PartitionSpec as P

LAGS = 512
SAMPLES = 512
TAPS = 32
FREQS = 384
PERIOD = 2 * FREQS
CH = 128
GROUP = 16
SPAN = 72
WIN = 128
LIMIT = 16 * 1024 * 1024
RING = 4
BF = jnp.bfloat16
F32 = jnp.float32


def split_bf16(matrix):
    high = matrix.astype(np.float32).astype(jnp.bfloat16)
    low = (matrix - high.astype(np.float64)).astype(np.float32).astype(jnp.bfloat16)
    return np.stack([high, low])


@functools.lru_cache(None)
def transforms():
    odd = 2 * np.arange(FREQS) + 1
    t = np.arange(SAMPLES)
    angle = np.pi / PERIOD * ((t[:, None] * odd[None, :]) % (2 * PERIOD))
    forward = np.stack([np.cos(angle), -np.sin(angle)], axis=1).reshape(SAMPLES, 2, -1, 128)
    forward = forward.transpose(0, 2, 1, 3).reshape(SAMPLES, PERIOD)
    lag = np.arange(LAGS) - LAGS // 2
    angle = np.pi / PERIOD * ((odd[:, None] * lag[None, :]) % (2 * PERIOD))
    back = np.stack([np.cos(angle), -np.sin(angle)], axis=0).reshape(2, -1, 128, LAGS)
    back = back.transpose(1, 0, 2, 3).reshape(PERIOD, LAGS) * (2.0 / PERIOD)
    return split_bf16(forward), split_bf16(back)


def device(src, z, y, core):
    return src * 32 + (z % RING) * 8 + (y % RING) * 2 + core


def owners():
    for s in range(4):
        for k in range(2):
            yield s, k, 2 * (s % 2), 2 * k + s // 2


def plans():
    first, side, along = [[], []], [], [[], [], []]
    for s, k, y, z in owners():

        def chip(own, across, core, s=s, k=k, y=y, z=z):
            return device(s, z + (across if k == 0 else own), y + (own if k == 0 else across), core)

        first[0].append((chip(0, 0, 0), chip(-1, 0, k)))
        first[1].append((chip(0, 0, 0), chip(2, 0, k)))
        first[1].append((chip(0, 0, 1), chip(1, 0, k)))
        side.append((chip(0, 0, 0), chip(0, 2, k)))
        side.append((chip(0, 0, 1), chip(0, 1, k)))
        for plan, d in zip(along, (2, 1, 3)):
            plan.extend((chip(i, 0, k), chip(i, d, k)) for i in range(0 if d == 3 else 1, RING))
    return first, side, along


def in_hbm(value):
    return pltpu.with_memory_space_constraint(value, pltpu.HBM)


def vmem(n):
    return [pl.BlockSpec(memory_space=pltpu.VMEM)] * n


def prefilter_kernel(
    traces_hbm, band_hbm, filters_hbm, w_ref, out_ref, near_ref, pad_ref, traces_ref, band_ref, filters_ref, sems
):
    pairs = ((traces_hbm, traces_ref), (band_hbm, band_ref), (filters_hbm, filters_ref))
    inputs = [pltpu.make_async_copy(a, b, sems.at[8 + i]) for i, (a, b) in enumerate(pairs)]
    for copy in inputs:
        copy.start()
    copies = [
        pltpu.make_async_copy(
            w_ref.at[i, pl.ds(j, 128)], near_ref.at[i, pl.ds(j, 128)], sems.at[4 * i + j // 128]
        )
        for i in range(2)
        for j in range(0, SAMPLES, 128)
    ]
    for copy in copies:
        copy.start()
    pad_ref[0:TAPS, :] = jnp.zeros((TAPS, CH), F32)
    for copy in inputs:
        copy.wait()
    bands = filters_ref.shape[0]
    onehot = (lax.broadcasted_iota(jnp.int32, (bands, CH), 0) == band_ref[...]).astype(F32)
    taps = lax.dot_general(
        filters_ref[...],
        onehot,
        (((0,), (0,)), ((), ())),
        precision=lax.Precision.HIGHEST,
        preferred_element_type=F32,
    )
    pad_ref[TAPS:, :] = traces_ref[...].astype(F32).T
    rows = 128
    power = jnp.zeros((1, CH), F32)
    parts = []
    for start in range(0, SAMPLES, rows):
        total = jnp.zeros((rows, CH), F32)
        for k in range(TAPS):
            low = TAPS + start - k
            total = total + taps[k : k + 1, :] * pad_ref[low : low + rows, :]
        power = power + jnp.sum(total * total, axis=0, keepdims=True)
        parts.append(total)
    scale = lax.rsqrt(power * (1.0 / SAMPLES) + 1e-06)
    for i, total in enumerate(parts):
        out_ref[:, i * rows : (i + 1) * rows] = (total * scale).T.astype(BF)
    for copy in copies:
        copy.wait()


def prefilter(traces, band_group, filters, w):
    return pl.pallas_call(
        prefilter_kernel,
        out_shape=[pltpu.VMEM((CH, SAMPLES), BF), pltpu.VMEM((2, SAMPLES, PERIOD), BF)],
        in_specs=[pl.BlockSpec(memory_space=pltpu.HBM)] * 4,
        out_specs=vmem(2),
        scratch_shapes=[
            pltpu.VMEM((TAPS + SAMPLES, CH), F32),
            pltpu.VMEM((CH, SAMPLES), BF),
            pltpu.VMEM((1, CH), jnp.int32),
            pltpu.VMEM(filters.shape, F32),
            pltpu.SemaphoreType.DMA((11,)),
        ],
        compiler_params=pltpu.CompilerParams(vmem_limit_bytes=LIMIT),
        name="prefilter",
    )(in_hbm(traces), in_hbm(band_group.reshape(1, CH)), in_hbm(filters), in_hbm(w))


def correlate_kernel(
    low_ref, held_ref, r0, r1, r2, r3, w_ref, fc_ref, bins_ref, hot_ref, pieces_ref, back_ref, out_ref,
    fs, total, wide,
):
    block = held_ref[...] + ((r0[...] + r1[...]) + (r2[...] + r3[...]))
    fs[...] = jnp.dot(block, w_ref[0], preferred_element_type=F32) + jnp.dot(
        block, w_ref[1], preferred_element_type=F32
    )
    total[...] = jnp.zeros_like(total)
    n_groups = CH // GROUP

    def spread(hot, j):
        return jnp.dot(hot, fc_ref[:, j * 256 : (j + 1) * 256], preferred_element_type=F32)

    def gather(g, j, span, buffer):
        first = pl.multiple_of(g * GROUP, GROUP)
        low = low_ref[g, 0]
        shift = low % 8
        start = pl.multiple_of(low - shift, 8)
        room = jnp.zeros((8, 128), F32)
        re, im = slice(j * 256, j * 256 + 128), slice(j * 256 + 128, (j + 1) * 256)
        fr, fi = fs[pl.ds(first, GROUP), re], fs[pl.ds(first, GROUP), im]
        sum_re = jnp.zeros((span, 128), F32)
        sum_im = jnp.zeros((span, 128), F32)
        for p in range(GROUP):
            rows = slice(p * span, (p + 1) * span)
            gr, gi = buffer[rows, 0:128], buffer[rows, 128:256]
            a, b = fr[p : p + 1, :], fi[p : p + 1, :]
            sum_re = sum_re + (a * gr + b * gi)
            sum_im = sum_im + (a * gi - b * gr)
        for part, value in ((re, sum_re), (im, sum_im)):
            moved = pltpu.roll(jnp.concatenate([value, room], axis=0), shift, 0)
            total[pl.ds(start, span + 8), part] += moved

    fits = low_ref[n_groups, 0] == 1

    @pl.when(fits)
    def _():
        def body(g, carry):
            for j in range(3):
                gather(g, j, SPAN, spread(hot_ref[g], j))
            return carry

        lax.fori_loop(0, n_groups, body, 0, unroll=4)

    @pl.when(jnp.logical_not(fits))
    def _():
        offsets = lax.broadcasted_iota(jnp.int32, (WIN, 2 * CH), 0)

        def body(g, carry):
            rel = bins_ref[pl.ds(pl.multiple_of(g * GROUP, GROUP), GROUP), :]
            for p in range(GROUP):
                row = jnp.where(rel[p : p + 1, :] == offsets, 1.0, 0.0)
                wide[p * WIN : (p + 1) * WIN, :] = row.astype(BF)
            for j in range(3):
                gather(g, j, WIN, spread(wide[...], j))
            return carry

        lax.fori_loop(0, n_groups, body, 0)

    for start in range(0, WIN, 128):
        value = total[start : start + 128, :]
        high = value.astype(BF)
        low = (value - high.astype(F32)).astype(BF)
        value = (
            jnp.dot(high, back_ref[0], preferred_element_type=F32)
            + jnp.dot(low, back_ref[0], preferred_element_type=F32)
            + jnp.dot(high, back_ref[1], preferred_element_type=F32)
        )
        out_ref[start : start + 128, :LAGS] = value.astype(BF)
    out_ref[:, LAGS:] = pieces_ref[...]


def correlate(lows, held, parts, w, fc, bins, hot, pieces, back):
    return pl.pallas_call(
        correlate_kernel,
        out_shape=jax.ShapeDtypeStruct((WIN, LAGS + 128), BF),
        in_specs=[pl.BlockSpec(memory_space=pltpu.SMEM)] + vmem(11),
        out_specs=pl.BlockSpec(memory_space=pltpu.VMEM),
        scratch_shapes=[
            pltpu.VMEM((CH, PERIOD), F32),
            pltpu.VMEM((2 * WIN, PERIOD), F32),
            pltpu.VMEM((GROUP * WIN, 2 * CH), BF),
        ],
        compiler_params=pltpu.CompilerParams(vmem_limit_bytes=LIMIT),
        cost_estimate=pl.CostEstimate(
            flops=2 * 128 * SPAN * 256 * PERIOD, bytes_accessed=6 * 1024 * 1024, transcendentals=0
        ),
        name="correlate",
    )(lows, held, *parts, w, fc, bins, hot, pieces, back)


def survey_kernel(
    scalars, pair_ref, other_ref, mine_ref, partner_ref, w_ref, bins_ref, table_ref, fc_ref, flag_ref, pieces_ref,
    raw, words, sem,
):
    core = scalars[0]
    copy = pltpu.make_async_copy(pair_ref.at[core], raw, sem)
    copy.start()
    flag_ref[...] = jnp.full(flag_ref.shape, scalars[1], jnp.int32)
    for i, ref in enumerate((mine_ref, partner_ref)):
        value = jnp.dot(ref[...], w_ref[0], preferred_element_type=F32)
        value = value + jnp.dot(ref[...], w_ref[1], preferred_element_type=F32)
        fc_ref[i * CH : (i + 1) * CH, :] = value.astype(BF)
    copy.wait()
    bins = jnp.concatenate([raw[...], other_ref[core]], axis=1)
    lowest = jnp.min(jnp.min(bins, axis=0, keepdims=True), axis=1, keepdims=True)
    rel = bins - lowest
    bins_ref[...] = rel
    n_groups = CH // GROUP
    grouped = rel.reshape(n_groups, GROUP, 2 * CH)
    low = jnp.min(jnp.min(grouped, axis=1), axis=1, keepdims=True)
    high = jnp.max(jnp.max(grouped, axis=1), axis=1, keepdims=True)
    widest = jnp.max(high - low, axis=0, keepdims=True)
    fits = (widest < SPAN).astype(jnp.int32)
    low = jnp.minimum(low * fits, WIN)
    table_ref[0:n_groups, :] = jnp.broadcast_to(low, (n_groups, 128))
    table_ref[n_groups:, :] = jnp.broadcast_to(fits, (8, 128))
    counts = tally_of(rel, words)
    lane = lax.broadcasted_iota(jnp.int32, (WIN, 128), 1) - 2 * core
    pieces = jnp.where(lane == 0, counts - counts % 256, 0) + jnp.where(lane == 1, counts % 256, 0)
    pieces_ref[...] = pieces.astype(F32).astype(BF)

def tally_of(rel, words):
    place = rel % 32
    unit = jnp.left_shift(1, rel // 32 * 8)

    def body(j, carry):
        hit = jnp.where(place == j, unit, 0)
        hit = hit[:, :CH] + hit[:, CH:]
        pieces = [hit[q : q + 8] for q in range(0, CH, 8)]
        while len(pieces) > 1:
            pieces = [x + y for x, y in zip(pieces[::2], pieces[1::2])]
        words[pl.ds(pl.multiple_of(j * 8, 8), 8), :] = pieces[0]
        return carry

    lax.fori_loop(0, 32, body, 0, unroll=4)
    packed = words[...]
    pieces = []
    for q in range(WIN // 32):
        part = jnp.bitwise_and(jnp.right_shift(packed, 8 * q), 255)
        part = jnp.sum(part.reshape(32, 8, CH), axis=1)
        pieces.append(jnp.sum(part, axis=1, keepdims=True))
    return jnp.concatenate(pieces, axis=0)


def survey(scalars, pair, other, mine, partner, w):
    whole = pl.BlockSpec(memory_space=pltpu.VMEM)
    far = pl.BlockSpec(memory_space=pltpu.HBM)
    return pl.pallas_call(
        survey_kernel,
        out_shape=[
            pltpu.VMEM((CH, 2 * CH), jnp.int32),
            jax.ShapeDtypeStruct((CH // GROUP + 8, 128), jnp.int32),
            pltpu.VMEM((2 * CH, PERIOD), BF),
            pltpu.VMEM((8, SAMPLES), jnp.int32),
            pltpu.VMEM((WIN, 128), BF),
        ],
        in_specs=[pl.BlockSpec(memory_space=pltpu.SMEM), far] + vmem(4),
        out_specs=[whole] * 5,
        scratch_shapes=[
            pltpu.VMEM((CH, CH), jnp.int32),
            pltpu.VMEM((32 * 8, CH), jnp.int32),
            pltpu.SemaphoreType.DMA,
        ],
        compiler_params=pltpu.CompilerParams(vmem_limit_bytes=LIMIT),
        cost_estimate=pl.CostEstimate(
            flops=2 * 2 * 2 * CH * SAMPLES * PERIOD, bytes_accessed=2 * 1024 * 1024, transcendentals=0
        ),
        name="survey",
    )(scalars, in_hbm(pair), other, mine, partner, w)


def prepare_kernel(
    scalars, low_ref, order_ref, pair_ref, other_ref, bins_ref, after_ref, hot_ref, pick_ref,
    ranks,
):
    core = scalars[0]
    columns = lax.broadcasted_iota(jnp.int32, (512, WIN), 1)
    turned = jnp.concatenate([order_ref[...], jnp.zeros((120, 128), jnp.int32)], axis=0).T
    ranks[...] = turned.reshape(8, 2, 8, 128)
    half = ranks[:, core].reshape(64, 128)
    order = jnp.concatenate([half[:, a : a + 1] for a in range(8)], axis=0)
    for i in range(2):
        step = core if i == 0 else 1 - core
        bins = jnp.concatenate([pair_ref[step], other_ref[step]], axis=1)
        lowest = jnp.min(jnp.min(bins, axis=0, keepdims=True), axis=1, keepdims=True)
        pick = jnp.where(order - lowest == columns, 1.0, 0.0).astype(BF)
        pick_ref[:, i * WIN : (i + 1) * WIN] = pick

    offsets = lax.broadcasted_iota(jnp.int32, (SPAN, 2 * CH), 0)

    def mark(g, carry):
        rel = bins_ref[pl.ds(pl.multiple_of(g * GROUP, GROUP), GROUP), :] - low_ref[g, 0]
        for p in range(0, GROUP, 2):
            hot_ref[g, p * SPAN : (p + 2) * SPAN, :] = jnp.concatenate(
                [jnp.where(rel[q : q + 1, :] == offsets, 1.0, 0.0) for q in (p, p + 1)], axis=0
            ).astype(BF)
        return carry

    lax.fori_loop(0, CH // GROUP, mark, 0)


def prepare(scalars, lows, order, pair, other, bins, after):
    return pl.pallas_call(
        prepare_kernel,
        out_shape=[
            pltpu.VMEM((CH // GROUP, GROUP * SPAN, 2 * CH), BF),
            pltpu.VMEM((512, 2 * WIN), BF),
        ],
        in_specs=[pl.BlockSpec(memory_space=pltpu.SMEM)] * 2 + vmem(4) + [pl.BlockSpec(memory_space=pl.ANY)],
        out_specs=vmem(2),
        scratch_shapes=[pltpu.VMEM((8, 2, 8, 128), jnp.int32)],
        compiler_params=pltpu.CompilerParams(vmem_limit_bytes=LIMIT),
        cost_estimate=pl.CostEstimate(flops=10**9, bytes_accessed=2**20, transcendentals=0),
        name="prepare",
    )(scalars, lows, order, pair, other, bins, after)


def arrange_kernel(pick_ref, mine_ref, other_ref, out_ref):
    window = jnp.concatenate([mine_ref[...], other_ref[...]], axis=0)
    out_ref[...] = jnp.dot(pick_ref[...], window, preferred_element_type=F32).astype(BF)


def arrange(pick, mine, other):
    return pl.pallas_call(
        arrange_kernel,
        out_shape=jax.ShapeDtypeStruct((512, LAGS + 128), BF),
        in_specs=vmem(3),
        out_specs=pl.BlockSpec(memory_space=pltpu.VMEM),
        compiler_params=pltpu.CompilerParams(vmem_limit_bytes=LIMIT),
        name="arrange",
    )(pick, mine, other)


def finish_kernel(parts_ref, out_ref):
    value = jnp.sum(parts_ref[...].astype(F32).reshape(64, 8, LAGS + 128), axis=0)
    totals = jnp.sum(value[:, LAGS:], axis=1, keepdims=True)
    out_ref[...] = value[:, :LAGS] / jnp.sqrt(SAMPLES * totals)


def finish(parts):
    return pl.pallas_call(
        finish_kernel,
        out_shape=jax.ShapeDtypeStruct((8, LAGS), F32),
        in_specs=vmem(1),
        out_specs=pl.BlockSpec(memory_space=pltpu.VMEM),
        compiler_params=pltpu.CompilerParams(vmem_limit_bytes=LIMIT),
        name="finish",
    )(parts)


def shards(traces, band_group, filters, pair_bin, bin_order):
    both = ("src", "rcv")
    swap = [(i, i ^ 1) for i in range(32)]
    forward, back = transforms()
    w, back = jnp.asarray(forward), jnp.asarray(back)
    src, rcv = lax.axis_index("src"), lax.axis_index("rcv")
    core = rcv % 2
    y, z = (rcv // 2) % RING, rcv // 8
    owner = jnp.logical_and(y == 2 * (src % 2), z == 2 * core + src // 2)
    scalars = jnp.stack([core, owner.astype(jnp.int32)])

    first, side, along = plans()
    other_pair = lax.ppermute(pair_bin, "rcv", swap)
    filtered, w = prefilter(traces, band_group, filters, w)
    filtered, other_pair = lax.optimization_barrier((filtered, other_pair))
    got = lax.ppermute(filtered, both, first[0])
    partner = lax.ppermute(filtered, "rcv", swap)
    seed = jnp.where(core == 0, filtered, partner)
    got = got + lax.ppermute(seed, both, first[1])
    parts = [lax.ppermute(seed, both, side)]
    bins, table, fc, flag, pieces = survey(scalars, pair_bin, other_pair, filtered, partner, w)
    held = jnp.where(flag[0:1] == 1, seed, got)
    parts = parts + [lax.ppermute(held, both, plan) for plan in along]
    hot, pick = prepare(
        scalars, table, bin_order.reshape(8, 128), pair_bin, other_pair, bins, held
    )

    window = correlate(table, held, parts, w, fc, bins, hot, pieces, back)
    other_window = lax.ppermute(window, "rcv", swap)
    payload = arrange(pick, window, other_window)
    groups = [[2 * i + c for i in range(64)] for c in range(2)]
    arrived = lax.all_to_all(payload, both, 0, 0, tiled=True, axis_index_groups=groups)
    return finish(arrived)


def solution(mesh):
    in_specs = (P("rcv", None), P("rcv"), P(), P(None, "src", "rcv"), P())
    out_specs = P(("src", "rcv"), None)
    return jax.shard_map(shards, mesh=mesh, in_specs=in_specs, out_specs=out_specs, check_vma=False)
```

```python
import functools

import jax
import jax.numpy as jnp
import numpy as np
from jax import lax
from jax.experimental import pallas as pl
from jax.experimental.pallas import tpu as pltpu
from jax.sharding import PartitionSpec as P

LAGS = 512
SAMPLES = 512
TAPS = 32
FREQS = 384
PERIOD = 2 * FREQS
CH = 128
GROUP = 16
SPAN = 72
WIN = 128
LIMIT = 16 * 1024 * 1024
RING = 4
BF = jnp.bfloat16
F32 = jnp.float32


def split_bf16(matrix):
    high = matrix.astype(np.float32).astype(jnp.bfloat16)
    low = (matrix - high.astype(np.float64)).astype(np.float32).astype(jnp.bfloat16)
    return np.stack([high, low])


@functools.lru_cache(None)
def transforms():
    odd = 2 * np.arange(FREQS) + 1
    t = np.arange(SAMPLES)
    angle = np.pi / PERIOD * ((t[:, None] * odd[None, :]) % (2 * PERIOD))
    forward = np.stack([np.cos(angle), -np.sin(angle)], axis=1).reshape(SAMPLES, 2, -1, 128)
    forward = forward.transpose(0, 2, 1, 3).reshape(SAMPLES, PERIOD)
    lag = np.arange(LAGS) - LAGS // 2
    angle = np.pi / PERIOD * ((odd[:, None] * lag[None, :]) % (2 * PERIOD))
    back = np.stack([np.cos(angle), -np.sin(angle)], axis=0).reshape(2, -1, 128, LAGS)
    back = back.transpose(1, 0, 2, 3).reshape(PERIOD, LAGS) * (2.0 / PERIOD)
    return split_bf16(forward), split_bf16(back)


def device(src, z, y, core):
    return src * 32 + (z % RING) * 8 + (y % RING) * 2 + core


def owners():
    for s in range(4):
        for k in range(2):
            yield s, k, 2 * (s % 2), 2 * k + s // 2


def plans():
    first, side, along = [[], []], [], [[], [], []]
    for s, k, y, z in owners():

        def chip(own, across, core, s=s, k=k, y=y, z=z):
            return device(s, z + (across if k == 0 else own), y + (own if k == 0 else across), core)

        first[0].append((chip(0, 0, 0), chip(-1, 0, k)))
        first[1].append((chip(0, 0, 0), chip(2, 0, k)))
        first[1].append((chip(0, 0, 1), chip(1, 0, k)))
        side.append((chip(0, 0, 0), chip(0, 2, k)))
        side.append((chip(0, 0, 1), chip(0, 1, k)))
        for plan, d in zip(along, (2, 1, 3) if k == 0 else (2, 3, 1)):
            plan.extend((chip(i, 0, k), chip(i, d, k)) for i in range(0 if d == 3 else 1, RING))
    return first, side, along


def in_hbm(value):
    return pltpu.with_memory_space_constraint(value, pltpu.HBM)


def vmem(n):
    return [pl.BlockSpec(memory_space=pltpu.VMEM)] * n


def prefilter_kernel(
    traces_hbm, band_hbm, filters_hbm, w_ref, out_ref, near_ref, pad_ref, traces_ref, band_ref, filters_ref, sems
):
    pairs = ((traces_hbm, traces_ref), (band_hbm, band_ref), (filters_hbm, filters_ref))
    inputs = [pltpu.make_async_copy(a, b, sems.at[8 + i]) for i, (a, b) in enumerate(pairs)]
    for copy in inputs:
        copy.start()
    copies = [
        pltpu.make_async_copy(
            w_ref.at[i, pl.ds(j, 128)], near_ref.at[i, pl.ds(j, 128)], sems.at[4 * i + j // 128]
        )
        for i in range(2)
        for j in range(0, SAMPLES, 128)
    ]
    for copy in copies:
        copy.start()
    pad_ref[0:TAPS, :] = jnp.zeros((TAPS, CH), F32)
    for copy in inputs:
        copy.wait()
    bands = filters_ref.shape[0]
    onehot = (lax.broadcasted_iota(jnp.int32, (bands, CH), 0) == band_ref[...]).astype(F32)
    taps = lax.dot_general(
        filters_ref[...],
        onehot,
        (((0,), (0,)), ((), ())),
        precision=lax.Precision.HIGHEST,
        preferred_element_type=F32,
    )
    pad_ref[TAPS:, :] = traces_ref[...].astype(F32).T
    rows = 128
    power = jnp.zeros((1, CH), F32)
    parts = []
    for start in range(0, SAMPLES, rows):
        total = jnp.zeros((rows, CH), F32)
        for k in range(TAPS):
            low = TAPS + start - k
            total = total + taps[k : k + 1, :] * pad_ref[low : low + rows, :]
        power = power + jnp.sum(total * total, axis=0, keepdims=True)
        parts.append(total)
    scale = lax.rsqrt(power * (1.0 / SAMPLES) + 1e-06)
    for i, total in enumerate(parts):
        out_ref[:, i * rows : (i + 1) * rows] = (total * scale).T.astype(BF)
    for copy in copies:
        copy.wait()


def prefilter(traces, band_group, filters, w):
    return pl.pallas_call(
        prefilter_kernel,
        out_shape=[pltpu.VMEM((CH, SAMPLES), BF), pltpu.VMEM((2, SAMPLES, PERIOD), BF)],
        in_specs=[pl.BlockSpec(memory_space=pltpu.HBM)] * 4,
        out_specs=vmem(2),
        scratch_shapes=[
            pltpu.VMEM((TAPS + SAMPLES, CH), F32),
            pltpu.VMEM((CH, SAMPLES), BF),
            pltpu.VMEM((1, CH), jnp.int32),
            pltpu.VMEM(filters.shape, F32),
            pltpu.SemaphoreType.DMA((11,)),
        ],
        compiler_params=pltpu.CompilerParams(vmem_limit_bytes=LIMIT),
        name="prefilter",
    )(in_hbm(traces), in_hbm(band_group.reshape(1, CH)), in_hbm(filters), in_hbm(w))


def correlate_kernel(
    low_ref, held_ref, r0, r1, r2, r3, w_ref, fc_ref, bins_ref, hot_ref, pieces_ref, back_ref, out_ref,
    fs, total, wide,
):
    block = held_ref[...] + ((r0[...] + r1[...]) + (r2[...] + r3[...]))
    fs[...] = jnp.dot(block, w_ref[0], preferred_element_type=F32) + jnp.dot(
        block, w_ref[1], preferred_element_type=F32
    )
    total[...] = jnp.zeros_like(total)
    n_groups = CH // GROUP

    def spread(hot, j):
        return jnp.dot(hot, fc_ref[:, j * 256 : (j + 1) * 256], preferred_element_type=F32)

    def gather(g, j, span, buffer):
        first = pl.multiple_of(g * GROUP, GROUP)
        low = low_ref[g, 0]
        shift = low % 8
        start = pl.multiple_of(low - shift, 8)
        room = jnp.zeros((8, 128), F32)
        re, im = slice(j * 256, j * 256 + 128), slice(j * 256 + 128, (j + 1) * 256)
        fr, fi = fs[pl.ds(first, GROUP), re], fs[pl.ds(first, GROUP), im]
        sum_re = jnp.zeros((span, 128), F32)
        sum_im = jnp.zeros((span, 128), F32)
        for p in range(GROUP):
            rows = slice(p * span, (p + 1) * span)
            gr, gi = buffer[rows, 0:128], buffer[rows, 128:256]
            a, b = fr[p : p + 1, :], fi[p : p + 1, :]
            sum_re = sum_re + (a * gr + b * gi)
            sum_im = sum_im + (a * gi - b * gr)
        for part, value in ((re, sum_re), (im, sum_im)):
            moved = pltpu.roll(jnp.concatenate([value, room], axis=0), shift, 0)
            total[pl.ds(start, span + 8), part] += moved

    fits = low_ref[n_groups, 0] == 1

    @pl.when(fits)
    def _():
        def body(g, carry):
            for j in range(3):
                gather(g, j, SPAN, spread(hot_ref[g], j))
            return carry

        lax.fori_loop(0, n_groups, body, 0, unroll=4)

    @pl.when(jnp.logical_not(fits))
    def _():
        offsets = lax.broadcasted_iota(jnp.int32, (WIN, 2 * CH), 0)

        def body(g, carry):
            rel = bins_ref[pl.ds(pl.multiple_of(g * GROUP, GROUP), GROUP), :]
            for p in range(GROUP):
                row = jnp.where(rel[p : p + 1, :] == offsets, 1.0, 0.0)
                wide[p * WIN : (p + 1) * WIN, :] = row.astype(BF)
            for j in range(3):
                gather(g, j, WIN, spread(wide[...], j))
            return carry

        lax.fori_loop(0, n_groups, body, 0)

    for start in range(0, WIN, 128):
        value = total[start : start + 128, :]
        high = value.astype(BF)
        low = (value - high.astype(F32)).astype(BF)
        value = (
            jnp.dot(high, back_ref[0], preferred_element_type=F32)
            + jnp.dot(low, back_ref[0], preferred_element_type=F32)
            + jnp.dot(high, back_ref[1], preferred_element_type=F32)
        )
        out_ref[start : start + 128, :LAGS] = value.astype(BF)
    out_ref[:, LAGS:] = pieces_ref[...]


def correlate(lows, held, parts, w, fc, bins, hot, pieces, back):
    return pl.pallas_call(
        correlate_kernel,
        out_shape=jax.ShapeDtypeStruct((WIN, LAGS + 128), BF),
        in_specs=[pl.BlockSpec(memory_space=pltpu.SMEM)] + vmem(11),
        out_specs=pl.BlockSpec(memory_space=pltpu.VMEM),
        scratch_shapes=[
            pltpu.VMEM((CH, PERIOD), F32),
            pltpu.VMEM((2 * WIN, PERIOD), F32),
            pltpu.VMEM((GROUP * WIN, 2 * CH), BF),
        ],
        compiler_params=pltpu.CompilerParams(vmem_limit_bytes=LIMIT),
        cost_estimate=pl.CostEstimate(
            flops=2 * 128 * SPAN * 256 * PERIOD, bytes_accessed=6 * 1024 * 1024, transcendentals=0
        ),
        name="correlate",
    )(lows, held, *parts, w, fc, bins, hot, pieces, back)


def survey_kernel(
    scalars, pair_ref, other_ref, mine_ref, partner_ref, w_ref, bins_ref, table_ref, fc_ref, flag_ref, pieces_ref,
    raw, words, sem,
):
    core = scalars[0]
    copy = pltpu.make_async_copy(pair_ref.at[core], raw, sem)
    copy.start()
    flag_ref[...] = jnp.full(flag_ref.shape, scalars[1], jnp.int32)
    for i, ref in enumerate((mine_ref, partner_ref)):
        value = jnp.dot(ref[...], w_ref[0], preferred_element_type=F32)
        value = value + jnp.dot(ref[...], w_ref[1], preferred_element_type=F32)
        fc_ref[i * CH : (i + 1) * CH, :] = value.astype(BF)
    copy.wait()
    bins = jnp.concatenate([raw[...], other_ref[core]], axis=1)
    lowest = jnp.min(jnp.min(bins, axis=0, keepdims=True), axis=1, keepdims=True)
    rel = bins - lowest
    bins_ref[...] = rel
    n_groups = CH // GROUP
    grouped = rel.reshape(n_groups, GROUP, 2 * CH)
    low = jnp.min(jnp.min(grouped, axis=1), axis=1, keepdims=True)
    high = jnp.max(jnp.max(grouped, axis=1), axis=1, keepdims=True)
    widest = jnp.max(high - low, axis=0, keepdims=True)
    fits = (widest < SPAN).astype(jnp.int32)
    low = jnp.minimum(low * fits, WIN)
    table_ref[0:n_groups, :] = jnp.broadcast_to(low, (n_groups, 128))
    table_ref[n_groups:, :] = jnp.broadcast_to(fits, (8, 128))
    counts = tally_of(rel, words)
    lane = lax.broadcasted_iota(jnp.int32, (WIN, 128), 1) - 2 * core
    pieces = jnp.where(lane == 0, counts - counts % 256, 0) + jnp.where(lane == 1, counts % 256, 0)
    pieces_ref[...] = pieces.astype(F32).astype(BF)

def tally_of(rel, words):
    place = rel % 32
    unit = jnp.left_shift(1, rel // 32 * 8)

    def body(j, carry):
        hit = jnp.where(place == j, unit, 0)
        hit = hit[:, :CH] + hit[:, CH:]
        pieces = [hit[q : q + 8] for q in range(0, CH, 8)]
        while len(pieces) > 1:
            pieces = [x + y for x, y in zip(pieces[::2], pieces[1::2])]
        words[pl.ds(pl.multiple_of(j * 8, 8), 8), :] = pieces[0]
        return carry

    lax.fori_loop(0, 32, body, 0, unroll=4)
    packed = words[...]
    pieces = []
    for q in range(WIN // 32):
        part = jnp.bitwise_and(jnp.right_shift(packed, 8 * q), 255)
        part = jnp.sum(part.reshape(32, 8, CH), axis=1)
        pieces.append(jnp.sum(part, axis=1, keepdims=True))
    return jnp.concatenate(pieces, axis=0)


def survey(scalars, pair, other, mine, partner, w):
    whole = pl.BlockSpec(memory_space=pltpu.VMEM)
    far = pl.BlockSpec(memory_space=pltpu.HBM)
    return pl.pallas_call(
        survey_kernel,
        out_shape=[
            pltpu.VMEM((CH, 2 * CH), jnp.int32),
            jax.ShapeDtypeStruct((CH // GROUP + 8, 128), jnp.int32),
            pltpu.VMEM((2 * CH, PERIOD), BF),
            pltpu.VMEM((8, SAMPLES), jnp.int32),
            pltpu.VMEM((WIN, 128), BF),
        ],
        in_specs=[pl.BlockSpec(memory_space=pltpu.SMEM), far] + vmem(4),
        out_specs=[whole] * 5,
        scratch_shapes=[
            pltpu.VMEM((CH, CH), jnp.int32),
            pltpu.VMEM((32 * 8, CH), jnp.int32),
            pltpu.SemaphoreType.DMA,
        ],
        compiler_params=pltpu.CompilerParams(vmem_limit_bytes=LIMIT),
        cost_estimate=pl.CostEstimate(
            flops=2 * 2 * 2 * CH * SAMPLES * PERIOD, bytes_accessed=2 * 1024 * 1024, transcendentals=0
        ),
        name="survey",
    )(scalars, in_hbm(pair), other, mine, partner, w)


def prepare_kernel(
    scalars, low_ref, order_ref, pair_ref, other_ref, bins_ref, after_ref, hot_ref, pick_ref,
    ranks,
):
    core = scalars[0]
    columns = lax.broadcasted_iota(jnp.int32, (512, WIN), 1)
    turned = jnp.concatenate([order_ref[...], jnp.zeros((120, 128), jnp.int32)], axis=0).T
    ranks[...] = turned.reshape(8, 2, 8, 128)
    half = ranks[:, core].reshape(64, 128)
    order = jnp.concatenate([half[:, a : a + 1] for a in range(8)], axis=0)
    for i in range(2):
        step = core if i == 0 else 1 - core
        bins = jnp.concatenate([pair_ref[step], other_ref[step]], axis=1)
        lowest = jnp.min(jnp.min(bins, axis=0, keepdims=True), axis=1, keepdims=True)
        pick = jnp.where(order - lowest == columns, 1.0, 0.0).astype(BF)
        pick_ref[:, i * WIN : (i + 1) * WIN] = pick

    offsets = lax.broadcasted_iota(jnp.int32, (SPAN, 2 * CH), 0)

    def mark(g, carry):
        rel = bins_ref[pl.ds(pl.multiple_of(g * GROUP, GROUP), GROUP), :] - low_ref[g, 0]
        for p in range(0, GROUP, 2):
            hot_ref[g, p * SPAN : (p + 2) * SPAN, :] = jnp.concatenate(
                [jnp.where(rel[q : q + 1, :] == offsets, 1.0, 0.0) for q in (p, p + 1)], axis=0
            ).astype(BF)
        return carry

    lax.fori_loop(0, CH // GROUP, mark, 0)


def prepare(scalars, lows, order, pair, other, bins, after):
    return pl.pallas_call(
        prepare_kernel,
        out_shape=[
            pltpu.VMEM((CH // GROUP, GROUP * SPAN, 2 * CH), BF),
            pltpu.VMEM((512, 2 * WIN), BF),
        ],
        in_specs=[pl.BlockSpec(memory_space=pltpu.SMEM)] * 2 + vmem(4) + [pl.BlockSpec(memory_space=pl.ANY)],
        out_specs=vmem(2),
        scratch_shapes=[pltpu.VMEM((8, 2, 8, 128), jnp.int32)],
        compiler_params=pltpu.CompilerParams(vmem_limit_bytes=LIMIT),
        cost_estimate=pl.CostEstimate(flops=10**9, bytes_accessed=2**20, transcendentals=0),
        name="prepare",
    )(scalars, lows, order, pair, other, bins, after)


def arrange_kernel(pick_ref, mine_ref, other_ref, out_ref):
    window = jnp.concatenate([mine_ref[...], other_ref[...]], axis=0)
    out_ref[...] = jnp.dot(pick_ref[...], window, preferred_element_type=F32).astype(BF)


def arrange(pick, mine, other):
    return pl.pallas_call(
        arrange_kernel,
        out_shape=jax.ShapeDtypeStruct((512, LAGS + 128), BF),
        in_specs=vmem(3),
        out_specs=pl.BlockSpec(memory_space=pltpu.VMEM),
        compiler_params=pltpu.CompilerParams(vmem_limit_bytes=LIMIT),
        name="arrange",
    )(pick, mine, other)


def finish_kernel(parts_ref, out_ref):
    value = jnp.sum(parts_ref[...].astype(F32).reshape(64, 8, LAGS + 128), axis=0)
    totals = jnp.sum(value[:, LAGS:], axis=1, keepdims=True)
    out_ref[...] = value[:, :LAGS] / jnp.sqrt(SAMPLES * totals)


def finish(parts):
    return pl.pallas_call(
        finish_kernel,
        out_shape=jax.ShapeDtypeStruct((8, LAGS), F32),
        in_specs=vmem(1),
        out_specs=pl.BlockSpec(memory_space=pltpu.VMEM),
        compiler_params=pltpu.CompilerParams(vmem_limit_bytes=LIMIT),
        name="finish",
    )(parts)


def shards(traces, band_group, filters, pair_bin, bin_order):
    both = ("src", "rcv")
    swap = [(i, i ^ 1) for i in range(32)]
    forward, back = transforms()
    w, back = jnp.asarray(forward), jnp.asarray(back)
    src, rcv = lax.axis_index("src"), lax.axis_index("rcv")
    core = rcv % 2
    y, z = (rcv // 2) % RING, rcv // 8
    owner = jnp.logical_and(y == 2 * (src % 2), z == 2 * core + src // 2)
    scalars = jnp.stack([core, owner.astype(jnp.int32)])

    first, side, along = plans()
    other_pair = lax.ppermute(pair_bin, "rcv", swap)
    filtered, w = prefilter(traces, band_group, filters, w)
    filtered, other_pair = lax.optimization_barrier((filtered, other_pair))
    got = lax.ppermute(filtered, both, first[0])
    partner = lax.ppermute(filtered, "rcv", swap)
    seed = jnp.where(core == 0, filtered, partner)
    got = got + lax.ppermute(seed, both, first[1])
    parts = [lax.ppermute(seed, both, side)]
    bins, table, fc, flag, pieces = survey(scalars, pair_bin, other_pair, filtered, partner, w)
    held = jnp.where(flag[0:1] == 1, seed, got)
    parts = parts + [lax.ppermute(held, both, plan) for plan in along]
    hot, pick = prepare(
        scalars, table, bin_order.reshape(8, 128), pair_bin, other_pair, bins, held
    )

    window = correlate(table, held, parts, w, fc, bins, hot, pieces, back)
    other_window = lax.ppermute(window, "rcv", swap)
    payload = arrange(pick, window, other_window)
    groups = [[2 * i + c for i in range(64)] for c in range(2)]
    arrived = lax.all_to_all(payload, both, 0, 0, tiled=True, axis_index_groups=groups)
    return finish(arrived)


def solution(mesh):
    in_specs = (P("rcv", None), P("rcv"), P(), P(None, "src", "rcv"), P())
    out_specs = P(("src", "rcv"), None)
    return jax.shard_map(shards, mesh=mesh, in_specs=in_specs, out_specs=out_specs, check_vma=False)
```
